256 devices in a mesh: seq: 8 (over z_lo, core), tile: 32 (over y, z_hi, x).
Axes of the slice: x: 4, y: 4, z: 8 (z_hi: 2, z_lo: 4; z = z_hi * 4 + z_lo), core: 2. Of those that a mesh axis runs over, the one named last changes fastest.
Arguments:
- queries: bfloat16 [16384, 2048], P(('seq', 'tile')), may hold values from -9 to 9
- keys: bfloat16 [16384, 2048], P(('seq', 'tile')), may hold values from -9 to 9
- values: bfloat16 [16384, 2048], P(('seq', 'tile')), may hold values from -6 to 6
- w_final: bfloat16 [2048, 64], replicated, may hold values from -12 to 12
- w_in: bfloat16 [3, 3, 3, 16, 256], replicated, may hold values from -0.3125 to 0.3125
- b_in: float32 [256], replicated, may hold values from -3 to 3
- w_out: bfloat16 [3, 3, 3, 256, 256], replicated, may hold values from -0.078125 to 0.078125
- b_out: float32 [256], replicated, may hold values from -3 to 3
Outputs:
- decoded: bfloat16 [16, 128, 128, 256], P('seq', None, 'tile')
The draws below stay inside these ranges and needn't reach their ends.
All inputs are finite; a program needn't handle non-finite values.
Results may differ from the reference program's by a relative error of at most 0.018.
Values may be sent and summed in bfloat16 or wider, within the bound.
No kernel may reach another device: no remote copies, remote signals or barrier semaphores. Data moves between devices by JAX's collectives and lax.ppermute only.
A program may use at most 64 MiB of HBM per device.

```python
import math
import jax
import jax.numpy as jnp
from jax import lax

HEADS = 16
HD = 128
LATC = 16
PATCH = 64
CH = 256
HT = 32
TOKENS = 16384
FT = 16
WT = 32


def draw_queries(key, part):
    key = jax.random.fold_in(key, 1)
    drawn = jnp.clip(jax.random.normal(key, (TOKENS, HEADS * HD), jnp.float32), -9.0, 9.0)
    return drawn.astype(jnp.bfloat16)


def draw_keys(key, part):
    key = jax.random.fold_in(key, 2)
    drawn = jnp.clip(jax.random.normal(key, (TOKENS, HEADS * HD), jnp.float32), -9.0, 9.0)
    return drawn.astype(jnp.bfloat16)


def block_levels(key, extent, shards, least, high):
    def one(position, parts):
        steps = jax.random.uniform(jax.random.fold_in(jax.random.fold_in(key, 6), position), (parts,), jnp.float32, least / len(shards), high / len(shards))
        return jnp.repeat(jnp.exp(steps), extent[position] // parts).reshape((-1,) + (1,) * (len(extent) - position - 1))

    gain = one(*shards[0])
    for cut in shards[1:]:
        gain = gain * one(*cut)
    return gain


def bell_draw(rng, dims, deviation, reach, cuts=(), kind=jnp.bfloat16):
    level = block_levels(rng, dims, cuts, -0.22, 0.18) if cuts else 1.0
    drawn = jax.random.normal(rng, dims, jnp.float32) * deviation * level
    return jnp.minimum(jnp.maximum(drawn, -reach), reach).astype(kind)


def setup_inputs(seed: int = 0) -> dict:
    streams_of = jax.random.split(jax.random.key(seed), 9)
    return {
        "queries": draw_queries(jax.random.fold_in(streams_of[8], 71), 0),
        "keys": draw_keys(jax.random.fold_in(streams_of[8], 71), 0),
        "values": bell_draw(streams_of[2], (TOKENS, HEADS * HD), 1.0, 6.0, ((0, 256),)),
        "w_final": bell_draw(streams_of[3], (HEADS * HD, PATCH), 2.0, 12.0),
        "w_in": bell_draw(streams_of[4], (3, 3, 3, LATC, CH), (27 * LATC) ** -0.5, 0.3125),
        "b_in": bell_draw(streams_of[5], (CH,), 0.5, 3.0, (), jnp.float32),
        "w_out": bell_draw(streams_of[6], (3, 3, 3, CH, CH), (27 * CH) ** -0.5, 0.078125),
        "b_out": bell_draw(streams_of[7], (CH,), 0.5, 3.0, (), jnp.float32),
    }


def attend_head(operands):
    head_q, head_k, head_v = operands
    block = math.gcd(512, TOKENS)
    scale = 1.0 / math.sqrt(HD)

    def query_block(block_q):
        scores = jnp.dot(block_q, head_k.T, preferred_element_type=jnp.float32) * scale
        largest = lax.optimization_barrier(jnp.max(scores, axis=-1, keepdims=True))
        expo = jnp.exp(scores - largest)
        total = lax.optimization_barrier(jnp.sum(expo, axis=-1, keepdims=True))
        weights = expo.astype(jnp.bfloat16)
        summed = jnp.dot(weights, head_v, preferred_element_type=jnp.float32)
        return (summed / total).astype(jnp.bfloat16)
    result = lax.map(query_block, head_q.reshape(TOKENS // block, block, HD))
    return result.reshape(TOKENS, HD)

def conv_full(padded, weight, frames, height, width_out):
    flat_w = weight.reshape(-1, weight.shape[-1])

    def one_frame(frame):
        window = lax.dynamic_slice_in_dim(padded, frame, 3, 0)
        pieces = []
        for step_t in range(3):
            for step_y in range(3):
                for step_x in range(3):
                    pieces.append(window[step_t, step_y:step_y + height, step_x:step_x + width_out])
        columns = jnp.concatenate(pieces, axis=-1)
        result = jnp.dot(columns.reshape(height * width_out, -1), flat_w, preferred_element_type=jnp.float32)
        return result.reshape(height, width_out, -1)
    return lax.map(one_frame, jnp.arange(frames, dtype=jnp.int32))

def reference(queries, keys, values, w_final, w_in, b_in, w_out, b_out):
    head_q = queries.reshape(TOKENS, HEADS, HD).transpose(1, 0, 2)
    head_k = keys.reshape(TOKENS, HEADS, HD).transpose(1, 0, 2)
    head_v = values.reshape(TOKENS, HEADS, HD).transpose(1, 0, 2)
    attended = lax.map(attend_head, (head_q, head_k, head_v))
    attended = attended.transpose(1, 0, 2).reshape(TOKENS, HEADS * HD)
    patch = jnp.dot(attended, w_final, preferred_element_type=jnp.float32).astype(jnp.bfloat16)
    latent = patch.reshape(FT, HT, WT, 2, 2, LATC).transpose(0, 1, 3, 2, 4, 5)
    latent = latent.reshape(FT, 2 * HT, 2 * WT, LATC)
    padded = jnp.pad(latent, ((2, 0), (1, 1), (1, 1), (0, 0)))
    first = (conv_full(padded, w_in, FT, 2 * HT, 2 * WT) + b_in).astype(jnp.bfloat16)
    upsampled = jnp.repeat(jnp.repeat(first, 2, axis=1), 2, axis=2)
    activated = jax.nn.silu(upsampled.astype(jnp.float32)).astype(jnp.bfloat16)
    padded_act = jnp.pad(activated, ((2, 0), (1, 1), (1, 1), (0, 0)))
    second = conv_full(padded_act, w_out, FT, 4 * HT, 4 * WT)
    return (upsampled.astype(jnp.float32) + second + b_out).astype(jnp.bfloat16)
```

```python
import functools
import math

import jax
import jax.numpy as jnp
from jax import lax
from jax.experimental import pallas as pl
from jax.experimental.pallas import tpu as pltpu
from jax.sharding import Mesh, PartitionSpec as P

AXES = ("zl", "core", "y", "zh", "x")
SIZES = (4, 2, 4, 2, 4)
PLANE = ("y", "x")
RING = ("zl", "zh")
STACK = ("zl", "core", "zh")

HEADS = 16
HD = 128
PW = 64
CH = 256
TOK = 64
MSG = 96
PLANE_TOK = 1024
SCALE = math.log2(math.e) / math.sqrt(HD)
BF = jnp.bfloat16
F32 = jnp.float32


def params():
    return pltpu.CompilerParams(vmem_limit_bytes=52 * 2**20)


def cost(flops, moved):
    return pl.CostEstimate(flops=flops, bytes_accessed=moved, transcendentals=0)


def pack_kv_kernel(k_ref, v_ref, w_ref, out_ref):
    for head in range(HEADS):
        lanes = pl.ds(head * HD, HD)
        out_ref[head, 0:TOK, :] = k_ref[:, lanes]
        small = jnp.dot(v_ref[:, lanes], w_ref[lanes, :], preferred_element_type=F32)
        packed = jnp.concatenate([small[: TOK // 2], small[TOK // 2 :]], axis=1)
        out_ref[head, TOK:MSG, :] = packed.astype(BF)


def pack_kv(keys, values, w_final):
    return pl.pallas_call(
        pack_kv_kernel,
        out_shape=jax.ShapeDtypeStruct((HEADS, MSG, HD), BF),
        compiler_params=params(),
        cost_estimate=cost(2 * TOK * HEADS * HD * PW, 2**20),
        name="pack_kv",
    )(keys, values, w_final)


def pack_q_kernel(q_ref, out_ref):
    for head in range(HEADS):
        out_ref[head] = q_ref[:, pl.ds(head * HD, HD)]


def pack_q(queries):
    return pl.pallas_call(
        pack_q_kernel,
        out_shape=jax.ShapeDtypeStruct((HEADS, TOK, HD), BF),
        compiler_params=params(),
        cost_estimate=cost(0, 2**19),
        name="pack_q",
    )(queries)


def attend_kernel(first, count, *refs):
    q_refs = refs[:2]
    kv_refs = refs[2 : 2 + count]
    old_ref = None if first else refs[2 + count]
    new_ref = refs[-1]

    def chunk(ref):
        rows = ref.shape[0] * TOK
        keys = ref[:, 0:TOK, :].reshape(rows, HD)
        packed = ref[:, TOK:MSG, :]
        small = jnp.concatenate([packed[:, :, :PW], packed[:, :, PW:]], axis=1).reshape(rows, PW)
        return keys, jnp.concatenate([small, jnp.ones_like(small)], axis=1)

    def scores(keys, q):
        s = lax.dot_general(keys, q, (((1,), (1,)), ((), ())), preferred_element_type=F32)
        return s.reshape(s.shape[0] // 8, 8, s.shape[1]) * SCALE

    def weighted(s, shift, wide):
        p = jnp.exp2(s - shift[None])
        p = p.reshape(s.shape[0] * 8, s.shape[2]).astype(BF)
        u = lax.dot_general(wide, p, (((0,), (0,)), ((), ())), preferred_element_type=F32)
        return u[PW : PW + 8], u[:PW]

    def top_of(s):
        return jnp.broadcast_to(jnp.max(jnp.max(s, axis=0), axis=0, keepdims=True), s.shape[1:])

    def start(side):
        if first:
            shift = top_of(scores(chunk(kv_refs[0])[0], q_refs[side][...]))
            return jnp.zeros((PW, shift.shape[1]), F32), jnp.zeros_like(shift), shift
        return old_ref[side, 0:PW], old_ref[side, PW : PW + 8], old_ref[side, PW + 8 : PW + 16]

    chunks = [chunk(ref) for ref in kv_refs]
    largest = jnp.float32(0)
    for side in range(2):
        q = q_refs[side][...]
        summed, total, shift = start(side)
        fresh = jnp.zeros_like(total)
        for keys, wide in chunks:
            t, u = weighted(scores(keys, q), shift, wide)
            fresh = fresh + t
            summed = summed + u
        new_ref[side, 0:PW] = summed
        new_ref[side, PW : PW + 8] = total + fresh
        new_ref[side, PW + 8 : PW + 16] = shift
        largest = jnp.maximum(largest, jnp.max(fresh))

    @pl.when(jnp.logical_not(largest <= 2.0**100))
    def _():
        for side in range(2):
            q = q_refs[side][...]
            summed, total, shift = start(side)
            top = shift
            for ref in kv_refs:
                top = jnp.maximum(top, top_of(scores(chunk(ref)[0], q)))
            shrink = jnp.exp2(shift - top)
            summed = summed * shrink[0:1]
            total = total * shrink
            for ref in kv_refs:
                keys, wide = chunk(ref)
                t, u = weighted(scores(keys, q), top, wide)
                total = total + t
                summed = summed + u
            new_ref[side, 0:PW] = summed
            new_ref[side, PW : PW + 8] = total
            new_ref[side, PW + 8 : PW + 16] = top


def attend(queries, messages, state):
    first = state is None
    operands = list(queries) + list(messages) + ([] if first else [state])
    rows = sum(item.shape[0] * TOK for item in messages)
    return pl.pallas_call(
        functools.partial(attend_kernel, first, len(messages)),
        out_shape=jax.ShapeDtypeStruct((2, PW + 16, PLANE_TOK), F32),
        compiler_params=params(),
        cost_estimate=cost(2 * 2 * PLANE_TOK * rows * 2 * HD, 2 * 2**20),
        name="attend",
    )(*operands)


def join_kernel(mine_ref, other_ref, out_ref, rows_ref):
    top = jnp.maximum(mine_ref[PW + 8 : PW + 16], other_ref[PW + 8 : PW + 16])
    one = jnp.exp2(mine_ref[PW + 8 : PW + 16] - top)
    two = jnp.exp2(other_ref[PW + 8 : PW + 16] - top)
    total = mine_ref[PW : PW + 8] * one + other_ref[PW : PW + 8] * two
    summed = mine_ref[0:PW] * one[0:1] + other_ref[0:PW] * two[0:1]
    share = summed / total[0:1]
    rows_ref[:, 0:PW] = jnp.transpose(share)
    none = jnp.zeros((32, PW), F32)
    columns = [rows_ref[pl.ds(c, 32, stride=32), 0:PW] for c in range(32)]

    def column(c):
        return columns[c] if 0 <= c < 32 else none

    for y in range(4):
        for x in range(4):
            for j in range(3):
                c = y * 8 + x - 1 + j
                both = jnp.concatenate([column(c), column(c + 4)], axis=1)
                out_ref[y * 4 + x, j] = both.astype(BF)


def join(mine, other):
    return pl.pallas_call(
        join_kernel,
        out_shape=jax.ShapeDtypeStruct((16, 3, 32, 2 * PW), BF),
        scratch_shapes=[pltpu.VMEM((PLANE_TOK, 2 * PW), F32)],
        compiler_params=params(),
        cost_estimate=cost(2**20, 2**20),
        name="join",
    )(mine, other)


def patch_kernel(in_ref, out_ref):
    total = in_ref[0].astype(F32)
    for head in range(1, HEADS):
        total = total + in_ref[head].astype(F32)
    for strip in range(2):
        part = total[:, :, strip * PW : (strip + 1) * PW]
        flat = jnp.concatenate([part[:, 0:16], part[:, 16:32]], axis=2).astype(BF)
        for group in range(8):
            out_ref[2 * group + strip] = flat


def patches(parts):
    return pl.pallas_call(
        patch_kernel,
        out_shape=jax.ShapeDtypeStruct((16, 3, 16, 2 * PW), BF),
        compiler_params=params(),
        cost_estimate=cost(2**19, 2**19),
        name="patch_sum",
    )(parts)


def fold_kernel(w_ref, out_ref):
    picks = {(0, 0): (0,), (0, 1): (1, 2), (1, 0): (0, 1), (1, 1): (2,)}
    for p in range(2):
        for i in range(2):
            rows = []
            for dx in range(3):
                row = w_ref[0, picks[p, i][0], dx].astype(F32)
                for dy in picks[p, i][1:]:
                    row = row + w_ref[0, dy, dx].astype(F32)
                rows.append(row)
            for q in range(2):
                for j in range(2):
                    tap = rows[picks[q, j][0]]
                    for dx in picks[q, j][1:]:
                        tap = tap + rows[dx]
                    out_ref[2 * p + q, 0, 2 * i + j] = tap.astype(BF)


def folded_weights(w_out):
    return pl.pallas_call(
        fold_kernel,
        grid=(3,),
        in_specs=[pl.BlockSpec((1, 3, 3, CH, CH), lambda d: (d, 0, 0, 0, 0))],
        out_specs=pl.BlockSpec((4, 1, 4, CH, CH), lambda d: (0, d, 0, 0, 0)),
        out_shape=jax.ShapeDtypeStruct((4, 3, 4, CH, CH), BF),
        compiler_params=params(),
        cost_estimate=cost(2**22, 10 * 2**20),
        name="fold_w_out",
    )(w_out)


def spread_weights(w_in):
    outer = []
    for a in range(2):
        inner = []
        for b in range(2):
            padded = jnp.pad(w_in, ((0, 0), (1 - a, a), (1 - b, b), (0, 0), (0, 0)))
            split = padded.reshape(3, 2, 2, 2, 2, 16, CH)
            inner.append(split.transpose(0, 1, 3, 2, 4, 5, 6).reshape(3 * 4 * PW, CH))
        outer.append(jnp.concatenate(inner, axis=1))
    return jnp.stack(outer)


def decode_kernel(where_ref, in_ref, w1_ref, b1_ref, w2_ref, b2_ref, out_ref, act_ref, res_ref):
    seq = where_ref[0]
    tile = where_ref[1]
    tokens = []
    for back in (2, 1, 0):
        source = jnp.maximum(seq - back, 0)
        known = (seq >= back).astype(F32)
        halves = [in_ref[2 * source + zh].astype(F32) * known for zh in range(2)]
        for frame in range(2):
            lanes = slice(frame * PW, (frame + 1) * PW)
            columns = []
            for j in range(3):
                pieces = []
                for high in range(2):
                    for zh in range(2):
                        pieces.append(halves[zh][j, high * 8 : (high + 1) * 8, lanes])
                columns.append(jnp.concatenate(pieces, axis=0))
            tokens.append(columns)
    blank = jnp.zeros((1, 2 * PW), F32)
    views = {}
    for frame in range(6):
        for side in range(2):
            both = jnp.concatenate([tokens[frame][side], tokens[frame][side + 1]], axis=1)
            views[frame, side, 0] = both.astype(BF)
            views[frame, side, -1] = jnp.concatenate([blank, both[:-1]], axis=0).astype(BF)
            views[frame, side, 1] = jnp.concatenate([both[1:], blank], axis=0).astype(BF)

    blank = jnp.zeros((1, CH), F32)
    first = {}
    for a in range(2):
        for side in range(2):
            rows = []
            for frame in range(4):
                row = []
                for dt in range(3):
                    for near in range(2):
                        row.append(views[frame + dt, side, a - 1 + near])
                rows.append(jnp.concatenate(row, axis=1))
            lhs = jnp.concatenate(rows, axis=0)
            got = jnp.dot(lhs, w1_ref[a], preferred_element_type=F32)
            for half in range(2):
                column = 2 * side + half
                b = 1 - half
                first[a, column] = (got[:, b * CH : (b + 1) * CH] + b1_ref[...]).astype(BF)

    for column in range(4):
        inside = 1.0
        if column == 0:
            inside = (tile > 0).astype(F32)
        if column == 3:
            inside = (tile < 31).astype(F32)
        for a in range(2):
            full = first[a, column].astype(F32)
            active = full / (1.0 + jnp.exp(-full))
            for frame in range(4):
                keep = inside * ((seq > 0).astype(F32) if frame < 2 else 1.0)
                part = active[frame * 32 : (frame + 1) * 32] * keep
                if a == 0:
                    act_ref[1, frame, column] = part.astype(BF)
                    act_ref[3, frame, column] = jnp.concatenate([part[1:], blank], 0).astype(BF)
                else:
                    act_ref[2, frame, column] = part.astype(BF)
                    act_ref[0, frame, column] = jnp.concatenate([blank, part[:-1]], 0).astype(BF)

    for p in range(2):
        for q in range(2):
            total = None
            for dt in range(3):
                for i in range(2):
                    for j in range(2):
                        blocks = []
                        for a in range(2):
                            view = act_ref[a + p + i, dt : dt + 2, q + j : q + j + 2]
                            blocks.append(view.reshape(128, CH))
                        lhs = jnp.concatenate(blocks, axis=0)
                        part = jnp.dot(lhs, w2_ref[2 * p + q, dt, 2 * i + j], preferred_element_type=F32)
                        total = part if total is None else total + part
            for a in range(2):
                for frame in range(2):
                    for column in range(2):
                        start = (a * 4 + frame * 2 + column) * 32
                        skip = first[a, column + 1][(frame + 2) * 32 : (frame + 3) * 32].astype(F32)
                        value = skip + total[start : start + 32] + b2_ref[...]
                        offset = frame * 512 + (2 * a + p) * 4 + 2 * column + q
                        for part in range(2):
                            res_ref[part, pl.ds(offset, 32, stride=16), :] = value[:, part * 128 : (part + 1) * 128]
    out_ref[:, 0:128] = res_ref[0].astype(BF)
    out_ref[:, 128:256] = res_ref[1].astype(BF)


def decode(where, patch, w1, b_in, w2, b_out):
    vmem = pl.BlockSpec(memory_space=pltpu.VMEM)
    return pl.pallas_call(
        decode_kernel,
        in_specs=[pl.BlockSpec(memory_space=pltpu.SMEM)] + [vmem] * 5,
        out_specs=vmem,
        out_shape=jax.ShapeDtypeStruct((1024, CH), BF),
        scratch_shapes=[pltpu.VMEM((4, 4, 4, 32, CH), BF), pltpu.VMEM((2, 1024, 128), F32)],
        compiler_params=params(),
        cost_estimate=cost(2 * 2**30, 10 * 2**20),
        name="decode",
    )(where, patch, w1, b_in.reshape(1, CH), w2, b_out.reshape(1, CH))


def around(step):
    def place(z):
        return (z % 4) * 2 + z // 4

    return [(place(z), place((z + step) % 8)) for z in range(8)]


def swapped(value, axes):
    return lax.all_to_all(value, axes, split_axis=0, concat_axis=0, tiled=True)


def shards(queries, keys, values, w_final, w_in, b_in, w_out, b_out):
    seq = lax.axis_index(("zl", "core")).astype(jnp.int32)
    tile = lax.axis_index(("y", "zh", "x")).astype(jnp.int32)
    where = jnp.stack([seq, tile])

    kv = swapped(pack_kv(keys, values, w_final), PLANE)
    halves = (kv[0:8], kv[8:16])
    ahead = list(halves)
    back = list(halves)
    arrived = []
    for hop in range(4):
        got = []
        for i in range(2):
            if hop < 3 or i == 0:
                ahead[i] = lax.ppermute(ahead[i], RING, around(1))
                got.append(ahead[i])
            if hop < 3 or i == 1:
                back[i] = lax.ppermute(back[i], RING, around(-1))
                got.append(back[i])
        arrived.append(got)

    own_q = swapped(pack_q(queries), PLANE).reshape(PLANE_TOK, HD)
    other_q = lax.ppermute(own_q, "core", [(0, 1), (1, 0)])
    both_q = (own_q, other_q)
    state = attend(both_q, halves, None)
    for got in arrived:
        state = attend(both_q, got, state)
    crossed = lax.ppermute(state[1], "core", [(0, 1), (1, 0)])
    parts = swapped(join(state[0], crossed), PLANE)
    patch = swapped(patches(parts), STACK)
    w1 = spread_weights(w_in)
    w2 = folded_weights(w_out)
    result = decode(where, patch, w1, b_in, w2, b_out)
    return result.reshape(2, 128, 4, CH)


def solution(mesh):
    fine = Mesh(mesh.devices.reshape(SIZES), AXES)
    tokens = P(AXES, None)
    placed = (tokens, tokens, tokens, P(), P(), P(), P(), P())
    return jax.shard_map(
        shards,
        mesh=fine,
        in_specs=placed,
        out_specs=P(("zl", "core"), None, ("y", "zh", "x"), None),
        check_vma=False,
    )
```

```python
import functools
import math

import jax
import jax.numpy as jnp
from jax import lax
from jax.experimental import pallas as pl
from jax.experimental.pallas import tpu as pltpu
from jax.sharding import Mesh, PartitionSpec as P

AXES = ("zl", "core", "y", "zh", "x")
SIZES = (4, 2, 4, 2, 4)
PLANE = ("y", "x")
STACK = ("zl", "core", "zh")

HEADS = 16
HD = 128
PW = 64
CH = 256
TOK = 64
MSG = 96
PLANE_TOK = 1024
SCALE = math.log2(math.e) / math.sqrt(HD)
BF = jnp.bfloat16
F32 = jnp.float32


def params(mib):
    return pltpu.CompilerParams(vmem_limit_bytes=mib * 2**20)


def cost(flops, moved):
    return pl.CostEstimate(flops=flops, bytes_accessed=moved, transcendentals=0)


def pack_kernel(q_hbm, k_hbm, v_hbm, w_hbm, out_ref, q_ref, k_ref, v_ref, w_ref, sems):
    moves = [
        pltpu.make_async_copy(source, target, sems.at[i])
        for i, (source, target) in enumerate(
            ((v_hbm, v_ref), (w_hbm, w_ref), (k_hbm, k_ref), (q_hbm, q_ref))
        )
    ]
    for move in moves:
        move.start()
    for move in moves[:2]:
        move.wait()
    for head in range(HEADS):
        lanes = pl.ds(head * HD, HD)
        small = lax.dot_general(
            v_ref[:, lanes], w_ref[:, lanes], (((1,), (1,)), ((), ())), preferred_element_type=F32
        )
        packed = jnp.concatenate([small[: TOK // 2], small[TOK // 2 :]], axis=1)
        out_ref[head, TOK:MSG] = packed.astype(BF)
    for move in moves[2:]:
        move.wait()
    for head in range(HEADS):
        lanes = pl.ds(head * HD, HD)
        out_ref[head, 0:TOK] = k_ref[:, lanes]
        out_ref[head, MSG : MSG + TOK] = q_ref[:, lanes]


def pack(queries, keys, values, w_final):
    return pl.pallas_call(
        pack_kernel,
        in_specs=[pl.BlockSpec(memory_space=pl.ANY)] * 4,
        out_shape=jax.ShapeDtypeStruct((HEADS, MSG + TOK, HD), BF),
        scratch_shapes=[pltpu.VMEM((TOK, HEADS * HD), BF)] * 3
        + [pltpu.VMEM((PW, HEADS * HD), BF), pltpu.SemaphoreType.DMA((4,))],
        compiler_params=params(60),
        cost_estimate=cost(2 * TOK * HEADS * HD * PW, 2**20),
        name="pack",
    )(queries, keys, values, w_final.T)


def attend_kernel(first, *refs):
    q_ref, kv_ref = refs[:2]
    old_ref = None if first else refs[2]
    new_ref, trial_ref, peak_ref = refs[-3:]
    sources = kv_ref.shape[0]

    def chunk(begin, count):
        rows = count * TOK
        keys = kv_ref[pl.ds(begin, count), 0:TOK, :].reshape(rows, HD)
        packed = kv_ref[pl.ds(begin, count), TOK:MSG, :]
        small = jnp.concatenate([packed[:, :, :PW], packed[:, :, PW:]], axis=1).reshape(rows, PW)
        return keys, jnp.concatenate([small, jnp.ones_like(small)], axis=1)

    def scores(keys, q):
        s = lax.dot_general(keys, q, (((1,), (1,)), ((), ())), preferred_element_type=F32)
        return s.reshape(s.shape[0] // 8, 8, s.shape[1]) * SCALE

    def weighted(s, shift, wide):
        p = jnp.exp2(s - shift[None])
        p = p.reshape(s.shape[0] * 8, s.shape[2]).astype(BF)
        u = lax.dot_general(wide, p, (((0,), (0,)), ((), ())), preferred_element_type=F32)
        return u[PW : PW + 8], u[:PW]

    def raise_peak(side, count):
        def more(i, _):
            s = scores(chunk(2 * i, 2)[0], q_ref[side])
            top = jnp.max(jnp.max(s, axis=0), axis=0, keepdims=True)
            peak_ref[...] = jnp.maximum(peak_ref[...], top)
            return 0

        lax.fori_loop(0, count // 2, more, 0)

    def attempt(side, largest):
        q = q_ref[side]
        if first:
            peak_ref[...] = jnp.full(peak_ref.shape, -jnp.inf, F32)
            raise_peak(side, 8)
            shift = peak_ref[...]
            total = jnp.zeros_like(shift)
            summed = jnp.zeros((PW, shift.shape[1]), F32)
        else:
            summed = old_ref[side, 0:PW]
            total = old_ref[side, PW : PW + 8]
            shift = old_ref[side, PW + 8 : PW + 16]
        fresh = jnp.zeros_like(total)
        for begin in range(0, sources, 8):
            keys, wide = chunk(begin, 8)
            t, u = weighted(scores(keys, q), shift, wide)
            fresh = fresh + t
            summed = summed + u
        trial_ref[side, 0:PW] = summed
        trial_ref[side, PW : PW + 8] = total + fresh
        trial_ref[side, PW + 8 : PW + 16] = shift
        return jnp.maximum(largest, jnp.max(fresh))

    largest = lax.fori_loop(0, q_ref.shape[0], attempt, jnp.float32(0))
    within = largest <= 2.0**100

    @pl.when(within)
    def _():
        new_ref[...] = trial_ref[...]

    @pl.when(jnp.logical_not(within))
    def _():
        def again(side, _):
            if first:
                new_ref[side] = jnp.zeros(new_ref.shape[1:], F32)
                shift = trial_ref[side, PW + 8 : PW + 16]
            else:
                new_ref[side] = old_ref[side]
                shift = new_ref[side, PW + 8 : PW + 16]
            peak_ref[...] = shift
            raise_peak(side, sources)
            top = peak_ref[...]
            shrink = jnp.exp2(shift - top)
            new_ref[side, 0:PW] = new_ref[side, 0:PW] * shrink[0:1]
            new_ref[side, PW : PW + 8] = new_ref[side, PW : PW + 8] * shrink
            new_ref[side, PW + 8 : PW + 16] = top

            def more(i, _):
                keys, wide = chunk(2 * i, 2)
                t, u = weighted(scores(keys, q_ref[side]), top, wide)
                new_ref[side, 0:PW] += u
                new_ref[side, PW : PW + 8] += t
                return 0

            return lax.fori_loop(0, sources // 2, more, 0)

        lax.fori_loop(0, q_ref.shape[0], again, 0)


def attend(queries, message, state):
    first = state is None
    operands = [queries, message] + ([] if first else [state])
    rows = message.shape[0] * TOK
    sides = queries.shape[0]
    return pl.pallas_call(
        functools.partial(attend_kernel, first),
        out_shape=jax.ShapeDtypeStruct((sides, PW + 16, PLANE_TOK), F32),
        scratch_shapes=[
            pltpu.VMEM((sides, PW + 16, PLANE_TOK), F32),
            pltpu.VMEM((8, PLANE_TOK), F32),
        ],
        input_output_aliases={} if first else {2: 0},
        compiler_params=params(20),
        cost_estimate=cost(2 * sides * PLANE_TOK * rows * 2 * HD, sides * 2**20),
        name="attend",
    )(*operands)


def join_kernel(mine_ref, other_ref, out_ref, rows_ref):
    top = jnp.maximum(mine_ref[PW + 8 : PW + 16], other_ref[PW + 8 : PW + 16])
    one = jnp.exp2(mine_ref[PW + 8 : PW + 16] - top)
    two = jnp.exp2(other_ref[PW + 8 : PW + 16] - top)
    total = mine_ref[PW : PW + 8] * one + other_ref[PW : PW + 8] * two
    summed = mine_ref[0:PW] * one[0:1] + other_ref[0:PW] * two[0:1]
    share = summed / total[0:1]
    rows_ref[:, 0:PW] = jnp.transpose(share)
    none = jnp.zeros((32, PW), F32)
    columns = [rows_ref[pl.ds(c, 32, stride=32), 0:PW] for c in range(32)]

    def column(c):
        return columns[c] if 0 <= c < 32 else none

    for y in range(4):
        for x in range(4):
            for j in range(3):
                c = y * 8 + x - 1 + j
                both = jnp.concatenate([column(c), column(c + 4)], axis=1)
                out_ref[y * 4 + x, j] = both.astype(BF)


def join(mine, other):
    return pl.pallas_call(
        join_kernel,
        out_shape=jax.ShapeDtypeStruct((16, 3, 32, 2 * PW), BF),
        scratch_shapes=[pltpu.VMEM((PLANE_TOK, 2 * PW), F32)],
        compiler_params=params(24),
        cost_estimate=cost(2**20, 2**20),
        name="join",
    )(mine, other)


def patch_kernel(in_ref, out_ref):
    total = in_ref[0].astype(F32)
    for head in range(1, HEADS):
        total = total + in_ref[head].astype(F32)
    for strip in range(2):
        part = total[:, :, strip * PW : (strip + 1) * PW]
        flat = jnp.concatenate([part[:, 0:16], part[:, 16:32]], axis=2).astype(BF)
        for group in range(8):
            out_ref[2 * group + strip] = flat


def patches(parts):
    return pl.pallas_call(
        patch_kernel,
        out_shape=jax.ShapeDtypeStruct((16, 3, 16, 2 * PW), BF),
        compiler_params=params(24),
        cost_estimate=cost(2**19, 2**19),
        name="patch_sum",
    )(parts)


def spread_w_in(w_ref, w1_ref):
    none = jnp.zeros((16, CH), BF)
    for a in range(2):
        for b in range(2):
            for near in range(4):
                for beside in range(4):
                    dy, dx = near - 1 + a, beside - 1 + b
                    place = ((near // 2) * 2 + beside // 2) * PW + ((near % 2) * 2 + beside % 2) * 16
                    for dt in range(3):
                        known = 0 <= dy < 3 and 0 <= dx < 3
                        tap = w_ref[dt, dy, dx] if known else none
                        rows = pl.ds(dt * 4 * PW + place, 16)
                        w1_ref[a, rows, b * CH : (b + 1) * CH] = tap


PICKS = {(0, 0): (0,), (0, 1): (1, 2), (1, 0): (0, 1), (1, 1): (2,)}


def fold_w_out(w_ref, w2_ref):
    def one(dt, _):
        for p in range(2):
            for i in range(2):
                rows = []
                for dx in range(3):
                    row = w_ref[dt, PICKS[p, i][0], dx].astype(F32)
                    for dy in PICKS[p, i][1:]:
                        row = row + w_ref[dt, dy, dx].astype(F32)
                    rows.append(row)
                for q in range(2):
                    for j in range(2):
                        tap = rows[PICKS[q, j][0]]
                        for dx in PICKS[q, j][1:]:
                            tap = tap + rows[dx]
                        w2_ref[2 * p + q, dt, 2 * i + j] = tap.astype(BF)
        return 0

    lax.fori_loop(0, 3, one, 0)


def decode_kernel(
    where_ref, in_ref, w_in_ref, b1_ref, w_out_ref, b2_ref, out_ref, act_ref, res_ref, w1_ref, w2_ref
):
    spread_w_in(w_in_ref, w1_ref)
    fold_w_out(w_out_ref, w2_ref)
    seq = where_ref[0]
    tile = where_ref[1]
    tokens = []
    for back in (2, 1, 0):
        source = jnp.maximum(seq - back, 0)
        known = (seq >= back).astype(F32)
        halves = [in_ref[2 * source + zh].astype(F32) * known for zh in range(2)]
        for frame in range(2):
            lanes = slice(frame * PW, (frame + 1) * PW)
            columns = []
            for j in range(3):
                pieces = []
                for high in range(2):
                    for zh in range(2):
                        pieces.append(halves[zh][j, high * 8 : (high + 1) * 8, lanes])
                columns.append(jnp.concatenate(pieces, axis=0))
            tokens.append(columns)
    blank = jnp.zeros((1, 2 * PW), F32)
    views = {}
    for frame in range(6):
        for side in range(2):
            both = jnp.concatenate([tokens[frame][side], tokens[frame][side + 1]], axis=1)
            views[frame, side, 0] = both.astype(BF)
            views[frame, side, -1] = jnp.concatenate([blank, both[:-1]], axis=0).astype(BF)
            views[frame, side, 1] = jnp.concatenate([both[1:], blank], axis=0).astype(BF)

    blank = jnp.zeros((1, CH), F32)
    first = {}
    for a in range(2):
        for side in range(2):
            rows = []
            for frame in range(4):
                row = []
                for dt in range(3):
                    for near in range(2):
                        row.append(views[frame + dt, side, a - 1 + near])
                rows.append(jnp.concatenate(row, axis=1))
            lhs = jnp.concatenate(rows, axis=0)
            got = jnp.dot(lhs, w1_ref[a], preferred_element_type=F32)
            for half in range(2):
                column = 2 * side + half
                b = 1 - half
                first[a, column] = (got[:, b * CH : (b + 1) * CH] + b1_ref[...]).astype(BF)

    for column in range(4):
        inside = 1.0
        if column == 0:
            inside = (tile > 0).astype(F32)
        if column == 3:
            inside = (tile < 31).astype(F32)
        for a in range(2):
            full = first[a, column].astype(F32)
            active = full / (1.0 + jnp.exp(-full))
            for frame in range(4):
                keep = inside * ((seq > 0).astype(F32) if frame < 2 else 1.0)
                part = active[frame * 32 : (frame + 1) * 32] * keep
                if a == 0:
                    act_ref[1, frame, column] = part.astype(BF)
                    act_ref[3, frame, column] = jnp.concatenate([part[1:], blank], 0).astype(BF)
                else:
                    act_ref[2, frame, column] = part.astype(BF)
                    act_ref[0, frame, column] = jnp.concatenate([blank, part[:-1]], 0).astype(BF)

    for p in range(2):
        for q in range(2):
            total = None
            for dt in range(3):
                for i in range(2):
                    for j in range(2):
                        blocks = []
                        for a in range(2):
                            view = act_ref[a + p + i, dt : dt + 2, q + j : q + j + 2]
                            blocks.append(view.reshape(128, CH))
                        lhs = jnp.concatenate(blocks, axis=0)
                        part = jnp.dot(lhs, w2_ref[2 * p + q, dt, 2 * i + j], preferred_element_type=F32)
                        total = part if total is None else total + part
            for a in range(2):
                for frame in range(2):
                    for column in range(2):
                        start = (a * 4 + frame * 2 + column) * 32
                        skip = first[a, column + 1][(frame + 2) * 32 : (frame + 3) * 32].astype(F32)
                        value = skip + total[start : start + 32] + b2_ref[...]
                        offset = frame * 512 + (2 * a + p) * 4 + 2 * column + q
                        for part in range(2):
                            res_ref[part, pl.ds(offset, 32, stride=16), :] = value[:, part * 128 : (part + 1) * 128]
    for part in range(2):
        for frame in range(2):
            block = res_ref[part, frame * 512 : (frame + 1) * 512].reshape(128, 4, 128)
            out_ref[frame, :, :, part * 128 : (part + 1) * 128] = block.astype(BF)


def decode(where, patch, w_in, b_in, w_out, b_out):
    vmem = pl.BlockSpec(memory_space=pltpu.VMEM)
    return pl.pallas_call(
        decode_kernel,
        in_specs=[pl.BlockSpec(memory_space=pltpu.SMEM)] + [vmem] * 5,
        out_specs=vmem,
        out_shape=jax.ShapeDtypeStruct((2, 128, 4, CH), BF),
        scratch_shapes=[
            pltpu.VMEM((4, 4, 4, 32, CH), BF),
            pltpu.VMEM((2, 1024, 128), F32),
            pltpu.VMEM((2, 12 * PW, 2 * CH), BF),
            pltpu.VMEM((4, 3, 4, CH, CH), BF),
        ],
        compiler_params=params(28),
        cost_estimate=cost(2 * 2**30, 10 * 2**20),
        name="decode",
    )(where, patch, w_in, b_in.reshape(1, CH), w_out, b_out.reshape(1, CH))


def around():
    pairs = []
    for core, step in ((0, 1), (1, -1)):
        for z in range(8):
            to = (z + step) % 8
            pairs.append(((z % 4) * 4 + core * 2 + z // 4, (to % 4) * 4 + core * 2 + to // 4))
    return pairs


def swapped(value, axes):
    return lax.all_to_all(value, axes, split_axis=0, concat_axis=0, tiled=True)


def hop(value):
    return lax.ppermute(value, STACK, around())


def across(value):
    return lax.ppermute(value, "core", [(0, 1), (1, 0)])


def shards(queries, keys, values, w_final, w_in, b_in, w_out, b_out):
    seq = lax.axis_index(("zl", "core")).astype(jnp.int32)
    tile = lax.axis_index(("y", "zh", "x")).astype(jnp.int32)
    where = jnp.stack([seq, tile])
    mixed = swapped(pack(queries, keys, values, w_final), PLANE)
    mine = mixed[:, 0:MSG]
    own_q = mixed[:, MSG:].reshape(PLANE_TOK, HD)
    both_q = jnp.stack([own_q, across(own_q)])
    state = attend(both_q, mine, None)
    first, second = hop(mine), hop(across(mine))
    for step in range(7):
        first, state, where = lax.optimization_barrier((first, state, where))
        message = first
        first, second = second, (hop(message) if step < 5 else None)
        if step < 6:
            state = attend(both_q, message, state)
    theirs = attend(both_q[1:2], message, state[1:2])
    theirs, kept_q, kept = lax.optimization_barrier((theirs, both_q[0:1], state[0:1]))
    crossed = across(theirs[0])
    ours = attend(kept_q, message, kept)
    parts = swapped(join(ours[0], crossed), PLANE)
    patch = swapped(patches(parts), STACK)
    return decode(where, patch, w_in, b_in, w_out, b_out)


def solution(mesh):
    fine = Mesh(mesh.devices.reshape(SIZES), AXES)
    tokens = P(AXES, None)
    placed = (tokens, tokens, tokens, P(), P(), P(), P(), P())
    return jax.shard_map(
        shards,
        mesh=fine,
        in_specs=placed,
        out_specs=P(("zl", "core"), None, ("y", "zh", "x"), None),
        check_vma=False,
    )
```

```python
import functools
import math

import jax
import jax.numpy as jnp
from jax import lax
from jax.experimental import pallas as pl
from jax.experimental.pallas import tpu as pltpu
from jax.sharding import Mesh, PartitionSpec as P

AXES = ("zl", "core", "y", "zh", "x")
SIZES = (4, 2, 4, 2, 4)
PLANE = ("y", "x")
STACK = ("zl", "core", "zh")

HEADS = 16
HD = 128
PW = 64
CH = 256
TOK = 64
MSG = 96
PLANE_TOK = 1024
SCALE = math.log2(math.e) / math.sqrt(HD)
BF = jnp.bfloat16
F32 = jnp.float32


def params(mib):
    return pltpu.CompilerParams(vmem_limit_bytes=mib * 2**20)


def cost(flops, moved):
    return pl.CostEstimate(flops=flops, bytes_accessed=moved, transcendentals=0)


def pack_kernel(q_hbm, k_hbm, v_hbm, w_hbm, out_ref, q_ref, k_ref, v_ref, w_ref, sems):
    moves = [
        pltpu.make_async_copy(source, target, sems.at[i])
        for i, (source, target) in enumerate(
            ((v_hbm, v_ref), (w_hbm, w_ref), (k_hbm, k_ref), (q_hbm, q_ref))
        )
    ]
    for move in moves:
        move.start()
    for move in moves[:2]:
        move.wait()
    for head in range(HEADS):
        lanes = pl.ds(head * HD, HD)
        small = lax.dot_general(
            v_ref[:, lanes], w_ref[:, lanes], (((1,), (1,)), ((), ())), preferred_element_type=F32
        )
        packed = jnp.concatenate([small[: TOK // 2], small[TOK // 2 :]], axis=1)
        out_ref[head, TOK:MSG] = packed.astype(BF)
    for move in moves[2:]:
        move.wait()
    for head in range(HEADS):
        lanes = pl.ds(head * HD, HD)
        out_ref[head, 0:TOK] = k_ref[:, lanes]
        out_ref[head, MSG : MSG + TOK] = q_ref[:, lanes]


def pack(queries, keys, values, w_final):
    return pl.pallas_call(
        pack_kernel,
        in_specs=[pl.BlockSpec(memory_space=pl.ANY)] * 4,
        out_shape=jax.ShapeDtypeStruct((HEADS, MSG + TOK, HD), BF),
        scratch_shapes=[pltpu.VMEM((TOK, HEADS * HD), BF)] * 3
        + [pltpu.VMEM((PW, HEADS * HD), BF), pltpu.SemaphoreType.DMA((4,))],
        compiler_params=params(60),
        cost_estimate=cost(2 * TOK * HEADS * HD * PW, 2**20),
        name="pack",
    )(queries, keys, values, w_final.T)


def attend_kernel(first, *refs):
    q_ref, kv_ref = refs[:2]
    old_ref = None if first else refs[2]
    new_ref, trial_ref, peak_ref = refs[-3:]
    sources = kv_ref.shape[0]

    def chunk(begin, count):
        rows = count * TOK
        keys = kv_ref[pl.ds(begin, count), 0:TOK, :].reshape(rows, HD)
        packed = kv_ref[pl.ds(begin, count), TOK:MSG, :]
        small = jnp.concatenate([packed[:, :, :PW], packed[:, :, PW:]], axis=1).reshape(rows, PW)
        return keys, jnp.concatenate([small, jnp.ones_like(small)], axis=1)

    def scores(keys, q):
        s = lax.dot_general(keys, q, (((1,), (1,)), ((), ())), preferred_element_type=F32)
        return s.reshape(s.shape[0] // 8, 8, s.shape[1]) * SCALE

    def weighted(s, shift, wide):
        p = jnp.exp2(s - shift[None])
        p = p.reshape(s.shape[0] * 8, s.shape[2]).astype(BF)
        u = lax.dot_general(wide, p, (((0,), (0,)), ((), ())), preferred_element_type=F32)
        return u[PW : PW + 8], u[:PW]

    def raise_peak(side, count):
        def more(i, _):
            s = scores(chunk(2 * i, 2)[0], q_ref[side])
            top = jnp.max(jnp.max(s, axis=0), axis=0, keepdims=True)
            peak_ref[...] = jnp.maximum(peak_ref[...], top)
            return 0

        lax.fori_loop(0, count // 2, more, 0)

    def attempt(side, largest):
        q = q_ref[side]
        if first:
            peak_ref[...] = jnp.full(peak_ref.shape, -jnp.inf, F32)
            raise_peak(side, 8)
            shift = peak_ref[...]
            total = jnp.zeros_like(shift)
            summed = jnp.zeros((PW, shift.shape[1]), F32)
        else:
            summed = old_ref[side, 0:PW]
            total = old_ref[side, PW : PW + 8]
            shift = old_ref[side, PW + 8 : PW + 16]
        fresh = jnp.zeros_like(total)
        for begin in range(0, sources, 8):
            keys, wide = chunk(begin, 8)
            t, u = weighted(scores(keys, q), shift, wide)
            fresh = fresh + t
            summed = summed + u
        trial_ref[side, 0:PW] = summed
        trial_ref[side, PW : PW + 8] = total + fresh
        trial_ref[side, PW + 8 : PW + 16] = shift
        return jnp.maximum(largest, jnp.max(fresh))

    largest = lax.fori_loop(0, q_ref.shape[0], attempt, jnp.float32(0))
    within = largest <= 2.0**100

    @pl.when(within)
    def _():
        new_ref[...] = trial_ref[...]

    @pl.when(jnp.logical_not(within))
    def _():
        def again(side, _):
            if first:
                new_ref[side] = jnp.zeros(new_ref.shape[1:], F32)
                shift = trial_ref[side, PW + 8 : PW + 16]
            else:
                new_ref[side] = old_ref[side]
                shift = new_ref[side, PW + 8 : PW + 16]
            peak_ref[...] = shift
            raise_peak(side, sources)
            top = peak_ref[...]
            shrink = jnp.exp2(shift - top)
            new_ref[side, 0:PW] = new_ref[side, 0:PW] * shrink[0:1]
            new_ref[side, PW : PW + 8] = new_ref[side, PW : PW + 8] * shrink
            new_ref[side, PW + 8 : PW + 16] = top

            def more(i, _):
                keys, wide = chunk(2 * i, 2)
                t, u = weighted(scores(keys, q_ref[side]), top, wide)
                new_ref[side, 0:PW] += u
                new_ref[side, PW : PW + 8] += t
                return 0

            return lax.fori_loop(0, sources // 2, more, 0)

        lax.fori_loop(0, q_ref.shape[0], again, 0)


def attend(queries, message, state):
    first = state is None
    operands = [queries, message] + ([] if first else [state])
    rows = message.shape[0] * TOK
    sides = queries.shape[0]
    return pl.pallas_call(
        functools.partial(attend_kernel, first),
        out_shape=jax.ShapeDtypeStruct((sides, PW + 16, PLANE_TOK), F32),
        scratch_shapes=[
            pltpu.VMEM((sides, PW + 16, PLANE_TOK), F32),
            pltpu.VMEM((8, PLANE_TOK), F32),
        ],
        input_output_aliases={} if first else {2: 0},
        compiler_params=params(20),
        cost_estimate=cost(2 * sides * PLANE_TOK * rows * 2 * HD, sides * 2**20),
        name="attend",
    )(*operands)


def join_kernel(mine_ref, other_ref, out_ref, rows_ref):
    top = jnp.maximum(mine_ref[PW + 8 : PW + 16], other_ref[PW + 8 : PW + 16])
    one = jnp.exp2(mine_ref[PW + 8 : PW + 16] - top)
    two = jnp.exp2(other_ref[PW + 8 : PW + 16] - top)
    total = mine_ref[PW : PW + 8] * one + other_ref[PW : PW + 8] * two
    summed = mine_ref[0:PW] * one[0:1] + other_ref[0:PW] * two[0:1]
    share = summed / total[0:1]
    rows_ref[:, 0:PW] = jnp.transpose(share)
    none = jnp.zeros((32, PW), F32)
    columns = [rows_ref[pl.ds(c, 32, stride=32), 0:PW] for c in range(32)]

    def column(c):
        return columns[c] if 0 <= c < 32 else none

    for y in range(4):
        for x in range(4):
            for j in range(3):
                c = y * 8 + x - 1 + j
                both = jnp.concatenate([column(c), column(c + 4)], axis=1)
                out_ref[y * 4 + x, j] = both.astype(BF)


def join(mine, other):
    return pl.pallas_call(
        join_kernel,
        out_shape=jax.ShapeDtypeStruct((16, 3, 32, 2 * PW), BF),
        scratch_shapes=[pltpu.VMEM((PLANE_TOK, 2 * PW), F32)],
        compiler_params=params(24),
        cost_estimate=cost(2**20, 2**20),
        name="join",
    )(mine, other)


def patch_kernel(in_ref, out_ref):
    total = in_ref[0].astype(F32)
    for head in range(1, HEADS):
        total = total + in_ref[head].astype(F32)
    for strip in range(2):
        part = total[:, :, strip * PW : (strip + 1) * PW]
        flat = jnp.concatenate([part[:, 0:16], part[:, 16:32]], axis=2).astype(BF)
        for group in range(8):
            out_ref[2 * group + strip] = flat


def patches(parts):
    return pl.pallas_call(
        patch_kernel,
        out_shape=jax.ShapeDtypeStruct((16, 3, 16, 2 * PW), BF),
        compiler_params=params(24),
        cost_estimate=cost(2**19, 2**19),
        name="patch_sum",
    )(parts)


def spread_w_in(w_ref, w1_ref):
    none = jnp.zeros((16, CH), BF)
    for a in range(2):
        for b in range(2):
            for near in range(4):
                for beside in range(4):
                    dy, dx = near - 1 + a, beside - 1 + b
                    place = ((near // 2) * 2 + beside // 2) * PW + ((near % 2) * 2 + beside % 2) * 16
                    for dt in range(3):
                        known = 0 <= dy < 3 and 0 <= dx < 3
                        tap = w_ref[dt, dy, dx] if known else none
                        rows = pl.ds(dt * 4 * PW + place, 16)
                        w1_ref[a, rows, b * CH : (b + 1) * CH] = tap


PICKS = {(0, 0): (0,), (0, 1): (1, 2), (1, 0): (0, 1), (1, 1): (2,)}


def upsampled_conv(w_ref, act_ref, sum_ref):
    def one(dt, _):
        for p in range(2):
            totals = [None, None]
            for i in range(2):
                rows = []
                for dx in range(3):
                    row = w_ref[dt, PICKS[p, i][0], dx].astype(F32)
                    for dy in PICKS[p, i][1:]:
                        row = row + w_ref[dt, dy, dx].astype(F32)
                    rows.append(row)
                for q in range(2):
                    for j in range(2):
                        tap = rows[PICKS[q, j][0]]
                        for dx in PICKS[q, j][1:]:
                            tap = tap + rows[dx]
                        blocks = []
                        for a in range(2):
                            view = act_ref[a + p + i, pl.ds(dt, 2), q + j : q + j + 2]
                            blocks.append(view.reshape(128, CH))
                        lhs = jnp.concatenate(blocks, axis=0)
                        part = jnp.dot(lhs, tap.astype(BF), preferred_element_type=F32)
                        totals[q] = part if totals[q] is None else totals[q] + part
            for q in range(2):
                sum_ref[2 * p + q] += totals[q]
        return 0

    sum_ref[...] = jnp.zeros(sum_ref.shape, F32)
    lax.fori_loop(0, 3, one, 0)


def decode_kernel(
    where_ref, in_ref, w_in_ref, b1_ref, w_out_ref, b2_ref, out_ref, act_ref, w1_ref, sum_ref
):
    spread_w_in(w_in_ref, w1_ref)
    seq = where_ref[0]
    tile = where_ref[1]
    tokens = []
    for back in (2, 1, 0):
        source = jnp.maximum(seq - back, 0)
        known = (seq >= back).astype(F32)
        halves = [in_ref[2 * source + zh].astype(F32) * known for zh in range(2)]
        for frame in range(2):
            lanes = slice(frame * PW, (frame + 1) * PW)
            columns = []
            for j in range(3):
                pieces = []
                for high in range(2):
                    for zh in range(2):
                        pieces.append(halves[zh][j, high * 8 : (high + 1) * 8, lanes])
                columns.append(jnp.concatenate(pieces, axis=0))
            tokens.append(columns)
    blank = jnp.zeros((1, 2 * PW), F32)
    views = {}
    for frame in range(6):
        for side in range(2):
            both = jnp.concatenate([tokens[frame][side], tokens[frame][side + 1]], axis=1)
            views[frame, side, 0] = both.astype(BF)
            views[frame, side, -1] = jnp.concatenate([blank, both[:-1]], axis=0).astype(BF)
            views[frame, side, 1] = jnp.concatenate([both[1:], blank], axis=0).astype(BF)

    blank = jnp.zeros((1, CH), F32)
    first = {}
    for a in range(2):
        for side in range(2):
            rows = []
            for frame in range(4):
                row = []
                for dt in range(3):
                    for near in range(2):
                        row.append(views[frame + dt, side, a - 1 + near])
                rows.append(jnp.concatenate(row, axis=1))
            lhs = jnp.concatenate(rows, axis=0)
            got = jnp.dot(lhs, w1_ref[a], preferred_element_type=F32)
            for half in range(2):
                column = 2 * side + half
                b = 1 - half
                first[a, column] = (got[:, b * CH : (b + 1) * CH] + b1_ref[...]).astype(BF)

    for column in range(4):
        inside = 1.0
        if column == 0:
            inside = (tile > 0).astype(F32)
        if column == 3:
            inside = (tile < 31).astype(F32)
        for a in range(2):
            full = first[a, column].astype(F32)
            active = full / (1.0 + jnp.exp(-full))
            for frame in range(4):
                keep = inside * ((seq > 0).astype(F32) if frame < 2 else 1.0)
                part = active[frame * 32 : (frame + 1) * 32] * keep
                if a == 0:
                    act_ref[1, frame, column] = part.astype(BF)
                    act_ref[3, frame, column] = jnp.concatenate([part[1:], blank], 0).astype(BF)
                else:
                    act_ref[2, frame, column] = part.astype(BF)
                    act_ref[0, frame, column] = jnp.concatenate([blank, part[:-1]], 0).astype(BF)

    upsampled_conv(w_out_ref, act_ref, sum_ref)
    to = lax.broadcasted_iota(jnp.int32, (256, 128), 0)
    source = lax.broadcasted_iota(jnp.int32, (256, 128), 1)
    order = jnp.where((to & 7) * 32 + (to >> 3) == source, 1.0, 0.0).astype(BF)
    for frame in range(2):
        for a in range(2):
            for p in range(2):
                columns = []
                for x in range(4):
                    column, q = x // 2, x % 2
                    start = (a * 4 + frame * 2 + column) * 32
                    skip = first[a, column + 1][(frame + 2) * 32 : (frame + 3) * 32].astype(F32)
                    columns.append(skip + sum_ref[2 * p + q, start : start + 32] + b2_ref[...])
                stacked = jnp.concatenate(columns, axis=0).astype(BF)
                rows = jnp.dot(order, stacked, preferred_element_type=F32)
                out_ref[frame, :, 2 * a + p] = rows.reshape(32, 8, CH)[:, 0:4].astype(BF)


def decode(where, patch, w_in, b_in, w_out, b_out):
    vmem = pl.BlockSpec(memory_space=pltpu.VMEM)
    return pl.pallas_call(
        decode_kernel,
        in_specs=[pl.BlockSpec(memory_space=pltpu.SMEM)] + [vmem] * 5,
        out_specs=vmem,
        out_shape=jax.ShapeDtypeStruct((2, 32, 4, 4, CH), BF),
        scratch_shapes=[
            pltpu.VMEM((4, 4, 4, 32, CH), BF),
            pltpu.VMEM((2, 12 * PW, 2 * CH), BF),
            pltpu.VMEM((4, 256, CH), F32),
        ],
        compiler_params=params(24),
        cost_estimate=cost(2 * 2**30, 10 * 2**20),
        name="decode",
    )(where, patch, w_in, b_in.reshape(1, CH), w_out, b_out.reshape(1, CH))


def around():
    pairs = []
    for core, step in ((0, 1), (1, -1)):
        for z in range(8):
            to = (z + step) % 8
            pairs.append(((z % 4) * 4 + core * 2 + z // 4, (to % 4) * 4 + core * 2 + to // 4))
    return pairs


def swapped(value, axes):
    return lax.all_to_all(value, axes, split_axis=0, concat_axis=0, tiled=True)


def hop(value):
    return lax.ppermute(value, STACK, around())


def across(value):
    return lax.ppermute(value, "core", [(0, 1), (1, 0)])


def shards(queries, keys, values, w_final, w_in, b_in, w_out, b_out):
    seq = lax.axis_index(("zl", "core")).astype(jnp.int32)
    tile = lax.axis_index(("y", "zh", "x")).astype(jnp.int32)
    where = jnp.stack([seq, tile])
    mixed = swapped(pack(queries, keys, values, w_final), PLANE)
    mine = mixed[:, 0:MSG]
    own_q = mixed[:, MSG:].reshape(PLANE_TOK, HD)
    both_q = jnp.stack([own_q, across(own_q)])
    state = attend(both_q, mine, None)
    coming = [hop(mine), hop(across(mine))]
    for step in range(6):
        message, state, where = lax.optimization_barrier((coming.pop(0), state, where))
        if step < 5:
            coming.append(hop(message))
        state = attend(both_q, message, state)
    message, state = lax.optimization_barrier((coming.pop(0), state))
    theirs = attend(both_q[1:2], message, state[1:2])
    theirs, kept_q, kept = lax.optimization_barrier((theirs, both_q[0:1], state[0:1]))
    crossed = across(theirs[0])
    ours = attend(kept_q, message, kept)
    parts = swapped(join(ours[0], crossed), PLANE)
    patch = swapped(patches(parts), STACK)
    return decode(where, patch, w_in, b_in, w_out, b_out).reshape(2, 128, 4, CH)


def solution(mesh):
    fine = Mesh(mesh.devices.reshape(SIZES), AXES)
    tokens = P(AXES, None)
    placed = (tokens, tokens, tokens, P(), P(), P(), P(), P())
    return jax.shard_map(
        shards,
        mesh=fine,
        in_specs=placed,
        out_specs=P(("zl", "core"), None, ("y", "zh", "x"), None),
        check_vma=False,
    )
```

```python
import functools
import math

import jax
import jax.numpy as jnp
from jax import lax
from jax.experimental import pallas as pl
from jax.experimental.pallas import tpu as pltpu
from jax.sharding import Mesh, PartitionSpec as P

AXES = ("zl", "core", "y", "zh", "x")
SIZES = (4, 2, 4, 2, 4)
PLANE = ("y", "x")
STACK = ("zl", "core", "zh")
RING = ("zl", "zh")

HEADS = 16
HD = 128
PW = 64
CH = 256
TOK = 64
MSG = 96
PLANE_TOK = 1024
SCALE = math.log2(math.e) / math.sqrt(HD)
BF = jnp.bfloat16
F32 = jnp.float32


def params(mib):
    return pltpu.CompilerParams(vmem_limit_bytes=mib * 2**20)


def cost(flops, moved):
    return pl.CostEstimate(flops=flops, bytes_accessed=moved, transcendentals=0)


def pack_kernel(q_hbm, k_hbm, v_hbm, w_hbm, out_ref, q_ref, k_ref, v_ref, w_ref, sems):
    moves = [
        pltpu.make_async_copy(source, target, sems.at[i])
        for i, (source, target) in enumerate(
            ((v_hbm, v_ref), (w_hbm, w_ref), (k_hbm, k_ref), (q_hbm, q_ref))
        )
    ]
    for move in moves:
        move.start()
    for move in moves[:2]:
        move.wait()
    for head in range(HEADS):
        lanes = pl.ds(head * HD, HD)
        small = lax.dot_general(
            v_ref[:, lanes], w_ref[:, lanes], (((1,), (1,)), ((), ())), preferred_element_type=F32
        )
        packed = jnp.concatenate([small[: TOK // 2], small[TOK // 2 :]], axis=1)
        out_ref[head, TOK:MSG] = packed.astype(BF)
    for move in moves[2:]:
        move.wait()
    for head in range(HEADS):
        lanes = pl.ds(head * HD, HD)
        out_ref[head, 0:TOK] = k_ref[:, lanes]
        out_ref[head, MSG : MSG + TOK] = q_ref[:, lanes]


def pack(queries, keys, values, w_final):
    return pl.pallas_call(
        pack_kernel,
        in_specs=[pl.BlockSpec(memory_space=pl.ANY)] * 4,
        out_shape=jax.ShapeDtypeStruct((HEADS, MSG + TOK, HD), BF),
        scratch_shapes=[pltpu.VMEM((TOK, HEADS * HD), BF)] * 3
        + [pltpu.VMEM((PW, HEADS * HD), BF), pltpu.SemaphoreType.DMA((4,))],
        compiler_params=params(60),
        cost_estimate=cost(2 * TOK * HEADS * HD * PW, 2**20),
        name="pack",
    )(queries, keys, values, w_final.T)


def attend_kernel(first, *refs):
    q_ref, kv_ref = refs[:2]
    old_ref = None if first else refs[2]
    new_ref, trial_ref, peak_ref = refs[-3:]
    sources = kv_ref.shape[0]

    def chunk(begin, count):
        rows = count * TOK
        keys = kv_ref[pl.ds(begin, count), 0:TOK, :].reshape(rows, HD)
        packed = kv_ref[pl.ds(begin, count), TOK:MSG, :]
        small = jnp.concatenate([packed[:, :, :PW], packed[:, :, PW:]], axis=1).reshape(rows, PW)
        return keys, jnp.concatenate([small, jnp.ones_like(small)], axis=1)

    def scores(keys, q):
        s = lax.dot_general(keys, q, (((1,), (1,)), ((), ())), preferred_element_type=F32)
        return s.reshape(s.shape[0] // 8, 8, s.shape[1]) * SCALE

    def weighted(s, shift, wide):
        p = jnp.exp2(s - shift[None])
        p = p.reshape(s.shape[0] * 8, s.shape[2]).astype(BF)
        u = lax.dot_general(wide, p, (((0,), (0,)), ((), ())), preferred_element_type=F32)
        return u[PW : PW + 8], u[:PW]

    def raise_peak(side, count):
        def more(i, _):
            s = scores(chunk(2 * i, 2)[0], q_ref[side])
            top = jnp.max(jnp.max(s, axis=0), axis=0, keepdims=True)
            peak_ref[...] = jnp.maximum(peak_ref[...], top)
            return 0

        lax.fori_loop(0, count // 2, more, 0)

    def attempt(side, largest):
        q = q_ref[side]
        if first:
            peak_ref[...] = jnp.full(peak_ref.shape, -jnp.inf, F32)
            raise_peak(side, 8)
            shift = peak_ref[...]
            total = jnp.zeros_like(shift)
            summed = jnp.zeros((PW, shift.shape[1]), F32)
        else:
            summed = old_ref[side, 0:PW]
            total = old_ref[side, PW : PW + 8]
            shift = old_ref[side, PW + 8 : PW + 16]
        fresh = jnp.zeros_like(total)
        for begin in range(0, sources, 8):
            keys, wide = chunk(begin, 8)
            t, u = weighted(scores(keys, q), shift, wide)
            fresh = fresh + t
            summed = summed + u
        trial_ref[side, 0:PW] = summed
        trial_ref[side, PW : PW + 8] = total + fresh
        trial_ref[side, PW + 8 : PW + 16] = shift
        return jnp.maximum(largest, jnp.max(fresh))

    largest = lax.fori_loop(0, q_ref.shape[0], attempt, jnp.float32(0))
    within = largest <= 2.0**100

    @pl.when(within)
    def _():
        new_ref[...] = trial_ref[...]

    @pl.when(jnp.logical_not(within))
    def _():
        def again(side, _):
            if first:
                new_ref[side] = jnp.zeros(new_ref.shape[1:], F32)
                shift = trial_ref[side, PW + 8 : PW + 16]
            else:
                new_ref[side] = old_ref[side]
                shift = new_ref[side, PW + 8 : PW + 16]
            peak_ref[...] = shift
            raise_peak(side, sources)
            top = peak_ref[...]
            shrink = jnp.exp2(shift - top)
            new_ref[side, 0:PW] = new_ref[side, 0:PW] * shrink[0:1]
            new_ref[side, PW : PW + 8] = new_ref[side, PW : PW + 8] * shrink
            new_ref[side, PW + 8 : PW + 16] = top

            def more(i, _):
                keys, wide = chunk(2 * i, 2)
                t, u = weighted(scores(keys, q_ref[side]), top, wide)
                new_ref[side, 0:PW] += u
                new_ref[side, PW : PW + 8] += t
                return 0

            return lax.fori_loop(0, sources // 2, more, 0)

        lax.fori_loop(0, q_ref.shape[0], again, 0)


def attend(queries, message, state):
    first = state is None
    operands = [queries, message] + ([] if first else [state])
    rows = message.shape[0] * TOK
    sides = queries.shape[0]
    return pl.pallas_call(
        functools.partial(attend_kernel, first),
        out_shape=jax.ShapeDtypeStruct((sides, PW + 16, PLANE_TOK), F32),
        scratch_shapes=[
            pltpu.VMEM((sides, PW + 16, PLANE_TOK), F32),
            pltpu.VMEM((8, PLANE_TOK), F32),
        ],
        input_output_aliases={} if first else {2: 0},
        compiler_params=params(20),
        cost_estimate=cost(2 * sides * PLANE_TOK * rows * 2 * HD, sides * 2**20),
        name="attend",
    )(*operands)


def join_kernel(mine_ref, other_ref, out_ref, rows_ref):
    top = jnp.maximum(mine_ref[PW + 8 : PW + 16], other_ref[PW + 8 : PW + 16])
    one = jnp.exp2(mine_ref[PW + 8 : PW + 16] - top)
    two = jnp.exp2(other_ref[PW + 8 : PW + 16] - top)
    total = mine_ref[PW : PW + 8] * one + other_ref[PW : PW + 8] * two
    summed = mine_ref[0:PW] * one[0:1] + other_ref[0:PW] * two[0:1]
    share = summed / total[0:1]
    rows_ref[:, 0:PW] = jnp.transpose(share)
    none = jnp.zeros((32, PW), F32)
    columns = [rows_ref[pl.ds(c, 32, stride=32), 0:PW] for c in range(32)]

    def column(c):
        return columns[c] if 0 <= c < 32 else none

    for y in range(4):
        for x in range(4):
            for j in range(3):
                c = y * 8 + x - 1 + j
                both = jnp.concatenate([column(c), column(c + 4)], axis=1)
                out_ref[y * 4 + x, j] = both.astype(BF)


def join(mine, other):
    return pl.pallas_call(
        join_kernel,
        out_shape=jax.ShapeDtypeStruct((16, 3, 32, 2 * PW), BF),
        scratch_shapes=[pltpu.VMEM((PLANE_TOK, 2 * PW), F32)],
        compiler_params=params(24),
        cost_estimate=cost(2**20, 2**20),
        name="join",
    )(mine, other)


def patch_kernel(in_ref, out_ref):
    total = in_ref[0].astype(F32)
    for head in range(1, HEADS):
        total = total + in_ref[head].astype(F32)
    for strip in range(2):
        part = total[:, :, strip * PW : (strip + 1) * PW]
        flat = jnp.concatenate([part[:, 0:16], part[:, 16:32]], axis=2).astype(BF)
        for group in range(4):
            out_ref[2 * group + strip] = flat


def patches(parts):
    return pl.pallas_call(
        patch_kernel,
        out_shape=jax.ShapeDtypeStruct((8, 3, 16, 2 * PW), BF),
        compiler_params=params(24),
        cost_estimate=cost(2**19, 2**19),
        name="patch_sum",
    )(parts)


def spread_w_in(w_ref, w1_ref):
    none = jnp.zeros((16, CH), BF)
    for a in range(2):
        for b in range(2):
            for near in range(4):
                for beside in range(4):
                    dy, dx = near - 1 + a, beside - 1 + b
                    place = ((near // 2) * 2 + beside // 2) * PW + ((near % 2) * 2 + beside % 2) * 16
                    for dt in range(3):
                        known = 0 <= dy < 3 and 0 <= dx < 3
                        tap = w_ref[dt, dy, dx] if known else none
                        rows = pl.ds(dt * 4 * PW + place, 16)
                        w1_ref[a, rows, b * CH : (b + 1) * CH] = tap


PICKS = {(0, 0): (0,), (0, 1): (1, 2), (1, 0): (0, 1), (1, 1): (2,)}


def upsampled_conv(w_ref, act_ref, sum_ref):
    def one(dt, _):
        for p in range(2):
            totals = [None, None]
            for i in range(2):
                rows = []
                for dx in range(3):
                    row = w_ref[dt, PICKS[p, i][0], dx].astype(F32)
                    for dy in PICKS[p, i][1:]:
                        row = row + w_ref[dt, dy, dx].astype(F32)
                    rows.append(row)
                for q in range(2):
                    for j in range(2):
                        tap = rows[PICKS[q, j][0]]
                        for dx in PICKS[q, j][1:]:
                            tap = tap + rows[dx]
                        blocks = []
                        for a in range(2):
                            view = act_ref[a + p + i, pl.ds(dt, 2), q + j : q + j + 2]
                            blocks.append(view.reshape(128, CH))
                        lhs = jnp.concatenate(blocks, axis=0)
                        part = jnp.dot(lhs, tap.astype(BF), preferred_element_type=F32)
                        totals[q] = part if totals[q] is None else totals[q] + part
            for q in range(2):
                sum_ref[2 * p + q] += totals[q]
        return 0

    sum_ref[...] = jnp.zeros(sum_ref.shape, F32)
    lax.fori_loop(0, 3, one, 0)


def decode_kernel(
    where_ref, own_ref, other_ref, w_in_ref, b1_ref, w_out_ref, b2_ref, out_ref, act_ref, w1_ref, sum_ref
):
    spread_w_in(w_in_ref, w1_ref)
    seq = where_ref[0]
    tile = where_ref[1]
    tokens = []
    for back in (2, 1, 0):
        chip = jnp.maximum(seq - back, 0) >> 1
        known = (seq >= back).astype(F32)
        in_ref = other_ref if back == 1 else own_ref
        halves = [in_ref[2 * chip + zh].astype(F32) * known for zh in range(2)]
        for frame in range(2):
            lanes = slice(frame * PW, (frame + 1) * PW)
            columns = []
            for j in range(3):
                pieces = []
                for high in range(2):
                    for zh in range(2):
                        pieces.append(halves[zh][j, high * 8 : (high + 1) * 8, lanes])
                columns.append(jnp.concatenate(pieces, axis=0))
            tokens.append(columns)
    blank = jnp.zeros((1, 2 * PW), F32)
    views = {}
    for frame in range(6):
        for side in range(2):
            both = jnp.concatenate([tokens[frame][side], tokens[frame][side + 1]], axis=1)
            views[frame, side, 0] = both.astype(BF)
            views[frame, side, -1] = jnp.concatenate([blank, both[:-1]], axis=0).astype(BF)
            views[frame, side, 1] = jnp.concatenate([both[1:], blank], axis=0).astype(BF)

    blank = jnp.zeros((1, CH), F32)
    first = {}
    for a in range(2):
        for side in range(2):
            rows = []
            for frame in range(4):
                row = []
                for dt in range(3):
                    for near in range(2):
                        row.append(views[frame + dt, side, a - 1 + near])
                rows.append(jnp.concatenate(row, axis=1))
            lhs = jnp.concatenate(rows, axis=0)
            got = jnp.dot(lhs, w1_ref[a], preferred_element_type=F32)
            for half in range(2):
                column = 2 * side + half
                b = 1 - half
                first[a, column] = (got[:, b * CH : (b + 1) * CH] + b1_ref[...]).astype(BF)

    for column in range(4):
        inside = 1.0
        if column == 0:
            inside = (tile > 0).astype(F32)
        if column == 3:
            inside = (tile < 31).astype(F32)
        for a in range(2):
            full = first[a, column].astype(F32)
            active = full / (1.0 + jnp.exp(-full))
            for frame in range(4):
                keep = inside * ((seq > 0).astype(F32) if frame < 2 else 1.0)
                part = active[frame * 32 : (frame + 1) * 32] * keep
                if a == 0:
                    act_ref[1, frame, column] = part.astype(BF)
                    act_ref[3, frame, column] = jnp.concatenate([part[1:], blank], 0).astype(BF)
                else:
                    act_ref[2, frame, column] = part.astype(BF)
                    act_ref[0, frame, column] = jnp.concatenate([blank, part[:-1]], 0).astype(BF)

    upsampled_conv(w_out_ref, act_ref, sum_ref)
    to = lax.broadcasted_iota(jnp.int32, (256, 128), 0)
    source = lax.broadcasted_iota(jnp.int32, (256, 128), 1)
    order = jnp.where((to & 7) * 32 + (to >> 3) == source, 1.0, 0.0).astype(BF)
    for frame in range(2):
        for a in range(2):
            for p in range(2):
                columns = []
                for x in range(4):
                    column, q = x // 2, x % 2
                    start = (a * 4 + frame * 2 + column) * 32
                    skip = first[a, column + 1][(frame + 2) * 32 : (frame + 3) * 32].astype(F32)
                    columns.append(skip + sum_ref[2 * p + q, start : start + 32] + b2_ref[...])
                stacked = jnp.concatenate(columns, axis=0).astype(BF)
                rows = jnp.dot(order, stacked, preferred_element_type=F32)
                out_ref[frame, :, 2 * a + p] = rows.reshape(32, 8, CH)[:, 0:4].astype(BF)


def decode(where, own, other, w_in, b_in, w_out, b_out):
    vmem = pl.BlockSpec(memory_space=pltpu.VMEM)
    return pl.pallas_call(
        decode_kernel,
        in_specs=[pl.BlockSpec(memory_space=pltpu.SMEM)] + [vmem] * 6,
        out_specs=vmem,
        out_shape=jax.ShapeDtypeStruct((2, 32, 4, 4, CH), BF),
        scratch_shapes=[
            pltpu.VMEM((4, 4, 4, 32, CH), BF),
            pltpu.VMEM((2, 12 * PW, 2 * CH), BF),
            pltpu.VMEM((4, 256, CH), F32),
        ],
        compiler_params=params(24),
        cost_estimate=cost(2 * 2**30, 10 * 2**20),
        name="decode",
    )(where, own, other, w_in, b_in.reshape(1, CH), w_out, b_out.reshape(1, CH))


def around():
    pairs = []
    for core, step in ((0, 1), (1, -1)):
        for z in range(8):
            to = (z + step) % 8
            pairs.append(((z % 4) * 4 + core * 2 + z // 4, (to % 4) * 4 + core * 2 + to // 4))
    return pairs


def swapped(value, axes):
    return lax.all_to_all(value, axes, split_axis=0, concat_axis=0, tiled=True)


def hop(value):
    return lax.ppermute(value, STACK, around())


def across(value):
    return lax.ppermute(value, "core", [(0, 1), (1, 0)])


def shards(queries, keys, values, w_final, w_in, b_in, w_out, b_out):
    seq = lax.axis_index(("zl", "core")).astype(jnp.int32)
    tile = lax.axis_index(("y", "zh", "x")).astype(jnp.int32)
    where = jnp.stack([seq, tile])
    mixed = swapped(pack(queries, keys, values, w_final), PLANE)
    mine = mixed[:, 0:MSG]
    own_q = mixed[:, MSG:].reshape(PLANE_TOK, HD)
    both_q = jnp.stack([own_q, across(own_q)])
    state = attend(both_q, mine, None)
    coming = [hop(mine), hop(across(mine))]
    for step in range(6):
        message, state, where = lax.optimization_barrier((coming.pop(0), state, where))
        if step < 5:
            coming.append(hop(message))
        state = attend(both_q, message, state)
    message, state = lax.optimization_barrier((coming.pop(0), state))
    theirs = attend(both_q[1:2], message, state[1:2])
    theirs, kept_q, kept = lax.optimization_barrier((theirs, both_q[0:1], state[0:1]))
    crossed = across(theirs[0])
    ours = attend(kept_q, message, kept)
    parts = swapped(join(ours[0], crossed), PLANE)
    patch = swapped(patches(parts), RING)
    return decode(where, patch, across(patch), w_in, b_in, w_out, b_out).reshape(2, 128, 4, CH)


def solution(mesh):
    fine = Mesh(mesh.devices.reshape(SIZES), AXES)
    tokens = P(AXES, None)
    placed = (tokens, tokens, tokens, P(), P(), P(), P(), P())
    return jax.shard_map(
        shards,
        mesh=fine,
        in_specs=placed,
        out_specs=P(("zl", "core"), None, ("y", "zh", "x"), None),
        check_vma=False,
    )
```

```python
import functools
import math

import jax
import jax.numpy as jnp
from jax import lax
from jax.experimental import pallas as pl
from jax.experimental.pallas import tpu as pltpu
from jax.sharding import Mesh, PartitionSpec as P

AXES = ("zl", "core", "y", "zh", "x")
SIZES = (4, 2, 4, 2, 4)
PLANE = ("y", "x")
STACK = ("zl", "core", "zh")
RING = ("zl", "zh")

HEADS = 16
HD = 128
PW = 64
CH = 256
TOK = 64
MSG = 96
PLANE_TOK = 1024
SCALE = math.log2(math.e) / math.sqrt(HD)
BF = jnp.bfloat16
F32 = jnp.float32


def params(mib):
    return pltpu.CompilerParams(vmem_limit_bytes=mib * 2**20)


def cost(flops, moved):
    return pl.CostEstimate(flops=flops, bytes_accessed=moved, transcendentals=0)


def pack_kernel(q_hbm, k_hbm, v_hbm, w_hbm, out_ref, q_ref, k_ref, v_ref, w_ref, sems):
    moves = [
        pltpu.make_async_copy(source, target, sems.at[i])
        for i, (source, target) in enumerate(
            ((v_hbm, v_ref), (w_hbm, w_ref), (k_hbm, k_ref), (q_hbm, q_ref))
        )
    ]
    for move in moves:
        move.start()
    for move in moves[:2]:
        move.wait()
    for head in range(HEADS):
        lanes = pl.ds(head * HD, HD)
        small = lax.dot_general(
            v_ref[:, lanes], w_ref[:, lanes], (((1,), (1,)), ((), ())), preferred_element_type=F32
        )
        packed = jnp.concatenate([small[: TOK // 2], small[TOK // 2 :]], axis=1)
        out_ref[head, TOK:MSG] = packed.astype(BF)
    for move in moves[2:]:
        move.wait()
    for head in range(HEADS):
        lanes = pl.ds(head * HD, HD)
        out_ref[head, 0:TOK] = k_ref[:, lanes]
        out_ref[head, MSG : MSG + TOK] = q_ref[:, lanes]


def pack(queries, keys, values, w_final):
    return pl.pallas_call(
        pack_kernel,
        in_specs=[pl.BlockSpec(memory_space=pl.ANY)] * 4,
        out_shape=jax.ShapeDtypeStruct((HEADS, MSG + TOK, HD), BF),
        scratch_shapes=[pltpu.VMEM((TOK, HEADS * HD), BF)] * 3
        + [pltpu.VMEM((PW, HEADS * HD), BF), pltpu.SemaphoreType.DMA((4,))],
        compiler_params=params(60),
        cost_estimate=cost(2 * TOK * HEADS * HD * PW, 2**20),
        name="pack",
    )(queries, keys, values, w_final.T)


def attend_kernel(first, *refs):
    q_ref, kv_ref = refs[:2]
    old_ref = None if first else refs[2]
    new_ref, trial_ref, peak_ref = refs[-3:]
    sources = kv_ref.shape[0]

    def chunk(begin, count):
        rows = count * TOK
        keys = kv_ref[pl.ds(begin, count), 0:TOK, :].reshape(rows, HD)
        packed = kv_ref[pl.ds(begin, count), TOK:MSG, :]
        small = jnp.concatenate([packed[:, :, :PW], packed[:, :, PW:]], axis=1).reshape(rows, PW)
        return keys, jnp.concatenate([small, jnp.ones_like(small)], axis=1)

    def scores(keys, q):
        s = lax.dot_general(keys, q, (((1,), (1,)), ((), ())), preferred_element_type=F32)
        return s.reshape(s.shape[0] // 8, 8, s.shape[1]) * SCALE

    def weighted(s, shift, wide):
        p = jnp.exp2(s - shift[None])
        p = p.reshape(s.shape[0] * 8, s.shape[2]).astype(BF)
        u = lax.dot_general(wide, p, (((0,), (0,)), ((), ())), preferred_element_type=F32)
        return u[PW : PW + 8], u[:PW]

    def raise_peak(side, count):
        def more(i, _):
            s = scores(chunk(2 * i, 2)[0], q_ref[side])
            top = jnp.max(jnp.max(s, axis=0), axis=0, keepdims=True)
            peak_ref[...] = jnp.maximum(peak_ref[...], top)
            return 0

        lax.fori_loop(0, count // 2, more, 0)

    def attempt(side, largest):
        q = q_ref[side]
        if first:
            peak_ref[...] = jnp.full(peak_ref.shape, -jnp.inf, F32)
            raise_peak(side, 8)
            shift = peak_ref[...]
            total = jnp.zeros_like(shift)
            summed = jnp.zeros((PW, shift.shape[1]), F32)
        else:
            summed = old_ref[side, 0:PW]
            total = old_ref[side, PW : PW + 8]
            shift = old_ref[side, PW + 8 : PW + 16]
        fresh = jnp.zeros_like(total)
        for begin in range(0, sources, 8):
            keys, wide = chunk(begin, 8)
            t, u = weighted(scores(keys, q), shift, wide)
            fresh = fresh + t
            summed = summed + u
        trial_ref[side, 0:PW] = summed
        trial_ref[side, PW : PW + 8] = total + fresh
        trial_ref[side, PW + 8 : PW + 16] = shift
        return jnp.maximum(largest, jnp.max(fresh))

    largest = lax.fori_loop(0, q_ref.shape[0], attempt, jnp.float32(0))
    within = largest <= 2.0**100

    @pl.when(within)
    def _():
        new_ref[...] = trial_ref[...]

    @pl.when(jnp.logical_not(within))
    def _():
        def again(side, _):
            if first:
                new_ref[side] = jnp.zeros(new_ref.shape[1:], F32)
                shift = trial_ref[side, PW + 8 : PW + 16]
            else:
                new_ref[side] = old_ref[side]
                shift = new_ref[side, PW + 8 : PW + 16]
            peak_ref[...] = shift
            raise_peak(side, sources)
            top = peak_ref[...]
            shrink = jnp.exp2(shift - top)
            new_ref[side, 0:PW] = new_ref[side, 0:PW] * shrink[0:1]
            new_ref[side, PW : PW + 8] = new_ref[side, PW : PW + 8] * shrink
            new_ref[side, PW + 8 : PW + 16] = top

            def more(i, _):
                keys, wide = chunk(2 * i, 2)
                t, u = weighted(scores(keys, q_ref[side]), top, wide)
                new_ref[side, 0:PW] += u
                new_ref[side, PW : PW + 8] += t
                return 0

            return lax.fori_loop(0, sources // 2, more, 0)

        lax.fori_loop(0, q_ref.shape[0], again, 0)


def attend(queries, message, state):
    first = state is None
    operands = [queries, message] + ([] if first else [state])
    rows = message.shape[0] * TOK
    sides = queries.shape[0]
    return pl.pallas_call(
        functools.partial(attend_kernel, first),
        out_shape=jax.ShapeDtypeStruct((sides, PW + 16, PLANE_TOK), F32),
        scratch_shapes=[
            pltpu.VMEM((sides, PW + 16, PLANE_TOK), F32),
            pltpu.VMEM((8, PLANE_TOK), F32),
        ],
        input_output_aliases={} if first else {2: 0},
        compiler_params=params(20),
        cost_estimate=cost(2 * sides * PLANE_TOK * rows * 2 * HD, sides * 2**20),
        name="attend",
    )(*operands)


def join_kernel(mine_ref, other_ref, out_ref, rows_ref):
    top = jnp.maximum(mine_ref[PW + 8 : PW + 16], other_ref[PW + 8 : PW + 16])
    one = jnp.exp2(mine_ref[PW + 8 : PW + 16] - top)
    two = jnp.exp2(other_ref[PW + 8 : PW + 16] - top)
    total = mine_ref[PW : PW + 8] * one + other_ref[PW : PW + 8] * two
    summed = mine_ref[0:PW] * one[0:1] + other_ref[0:PW] * two[0:1]
    share = summed / total[0:1]
    rows_ref[:, 0:PW] = jnp.transpose(share)
    none = jnp.zeros((32, PW), F32)
    columns = [rows_ref[pl.ds(c, 32, stride=32), 0:PW] for c in range(32)]

    def column(c):
        return columns[c] if 0 <= c < 32 else none

    for y in range(4):
        for x in range(4):
            for j in range(3):
                c = y * 8 + x - 1 + j
                both = jnp.concatenate([column(c), column(c + 4)], axis=1)
                out_ref[y * 4 + x, j] = both.astype(BF)


def join(mine, other):
    return pl.pallas_call(
        join_kernel,
        out_shape=jax.ShapeDtypeStruct((16, 3, 32, 2 * PW), BF),
        scratch_shapes=[pltpu.VMEM((PLANE_TOK, 2 * PW), F32)],
        compiler_params=params(24),
        cost_estimate=cost(2**20, 2**20),
        name="join",
    )(mine, other)


def patch_kernel(in_ref, out_ref):
    total = in_ref[0].astype(F32)
    for head in range(1, HEADS):
        total = total + in_ref[head].astype(F32)
    for strip in range(2):
        part = total[:, :, strip * PW : (strip + 1) * PW]
        flat = jnp.concatenate([part[:, 0:16], part[:, 16:32]], axis=2).astype(BF)
        for group in range(4):
            out_ref[2 * group + strip] = flat


def patches(parts):
    return pl.pallas_call(
        patch_kernel,
        out_shape=jax.ShapeDtypeStruct((8, 3, 16, 2 * PW), BF),
        compiler_params=params(24),
        cost_estimate=cost(2**19, 2**19),
        name="patch_sum",
    )(parts)


def spread_w_in(w_ref, w1_ref):
    none = jnp.zeros((16, CH), BF)
    for a in range(2):
        for b in range(2):
            for near in range(4):
                for beside in range(4):
                    dy, dx = near - 1 + a, beside - 1 + b
                    place = ((near // 2) * 2 + beside // 2) * PW + ((near % 2) * 2 + beside % 2) * 16
                    for dt in range(3):
                        known = 0 <= dy < 3 and 0 <= dx < 3
                        tap = w_ref[dt, dy, dx] if known else none
                        rows = pl.ds(dt * 4 * PW + place, 16)
                        w1_ref[a, rows, b * CH : (b + 1) * CH] = tap


PICKS = {(0, 0): (0,), (0, 1): (1, 2), (1, 0): (0, 1), (1, 1): (2,)}


def upsampled_conv(w_ref, act_ref, sum_ref):
    for p in range(2):
        totals = [None, None]
        for dt in range(3):
            for i in range(2):
                rows = []
                for dx in range(3):
                    row = w_ref[dt, PICKS[p, i][0], dx].astype(F32)
                    for dy in PICKS[p, i][1:]:
                        row = row + w_ref[dt, dy, dx].astype(F32)
                    rows.append(row)
                for q in range(2):
                    for j in range(2):
                        tap = rows[PICKS[q, j][0]]
                        for dx in PICKS[q, j][1:]:
                            tap = tap + rows[dx]
                        blocks = []
                        for a in range(2):
                            view = act_ref[a + p + i, dt : dt + 2, q + j : q + j + 2]
                            blocks.append(view.reshape(128, CH))
                        lhs = jnp.concatenate(blocks, axis=0)
                        part = jnp.dot(lhs, tap.astype(BF), preferred_element_type=F32)
                        totals[q] = part if totals[q] is None else totals[q] + part
        for q in range(2):
            sum_ref[2 * p + q] = totals[q]


def decode_kernel(
    where_ref, own_ref, other_ref, w_in_ref, b1_ref, w_out_ref, b2_ref, out_ref, act_ref, w1_ref, sum_ref
):
    spread_w_in(w_in_ref, w1_ref)
    seq = where_ref[0]
    tile = where_ref[1]
    tokens = []
    for back in (2, 1, 0):
        chip = jnp.maximum(seq - back, 0) >> 1
        known = (seq >= back).astype(F32)
        in_ref = other_ref if back == 1 else own_ref
        halves = [in_ref[2 * chip + zh].astype(F32) * known for zh in range(2)]
        for frame in range(2):
            lanes = slice(frame * PW, (frame + 1) * PW)
            columns = []
            for j in range(3):
                pieces = []
                for high in range(2):
                    for zh in range(2):
                        pieces.append(halves[zh][j, high * 8 : (high + 1) * 8, lanes])
                columns.append(jnp.concatenate(pieces, axis=0))
            tokens.append(columns)
    blank = jnp.zeros((1, 2 * PW), F32)
    views = {}
    for frame in range(6):
        for side in range(2):
            both = jnp.concatenate([tokens[frame][side], tokens[frame][side + 1]], axis=1)
            views[frame, side, 0] = both.astype(BF)
            views[frame, side, -1] = jnp.concatenate([blank, both[:-1]], axis=0).astype(BF)
            views[frame, side, 1] = jnp.concatenate([both[1:], blank], axis=0).astype(BF)

    blank = jnp.zeros((1, CH), F32)
    first = {}
    for a in range(2):
        for side in range(2):
            rows = []
            for frame in range(4):
                row = []
                for dt in range(3):
                    for near in range(2):
                        row.append(views[frame + dt, side, a - 1 + near])
                rows.append(jnp.concatenate(row, axis=1))
            lhs = jnp.concatenate(rows, axis=0)
            got = jnp.dot(lhs, w1_ref[a], preferred_element_type=F32)
            for half in range(2):
                column = 2 * side + half
                b = 1 - half
                first[a, column] = (got[:, b * CH : (b + 1) * CH] + b1_ref[...]).astype(BF)

    for column in range(4):
        inside = 1.0
        if column == 0:
            inside = (tile > 0).astype(F32)
        if column == 3:
            inside = (tile < 31).astype(F32)
        for a in range(2):
            full = first[a, column].astype(F32)
            active = full / (1.0 + jnp.exp(-full))
            for frame in range(4):
                keep = inside * ((seq > 0).astype(F32) if frame < 2 else 1.0)
                part = active[frame * 32 : (frame + 1) * 32] * keep
                if a == 0:
                    act_ref[1, frame, column] = part.astype(BF)
                    act_ref[3, frame, column] = jnp.concatenate([part[1:], blank], 0).astype(BF)
                else:
                    act_ref[2, frame, column] = part.astype(BF)
                    act_ref[0, frame, column] = jnp.concatenate([blank, part[:-1]], 0).astype(BF)

    upsampled_conv(w_out_ref, act_ref, sum_ref)
    to = lax.broadcasted_iota(jnp.int32, (256, 128), 0)
    source = lax.broadcasted_iota(jnp.int32, (256, 128), 1)
    order = jnp.where((to & 7) * 32 + (to >> 3) == source, 1.0, 0.0).astype(BF)
    for frame in range(2):
        for a in range(2):
            for p in range(2):
                columns = []
                for x in range(4):
                    column, q = x // 2, x % 2
                    start = (a * 4 + frame * 2 + column) * 32
                    skip = first[a, column + 1][(frame + 2) * 32 : (frame + 3) * 32].astype(F32)
                    columns.append(skip + sum_ref[2 * p + q, start : start + 32] + b2_ref[...])
                stacked = jnp.concatenate(columns, axis=0).astype(BF)
                rows = jnp.dot(order, stacked, preferred_element_type=F32)
                out_ref[frame, :, 2 * a + p] = rows.reshape(32, 8, CH)[:, 0:4].astype(BF)


def decode(where, own, other, w_in, b_in, w_out, b_out):
    vmem = pl.BlockSpec(memory_space=pltpu.VMEM)
    return pl.pallas_call(
        decode_kernel,
        in_specs=[pl.BlockSpec(memory_space=pltpu.SMEM)] + [vmem] * 6,
        out_specs=vmem,
        out_shape=jax.ShapeDtypeStruct((2, 32, 4, 4, CH), BF),
        scratch_shapes=[
            pltpu.VMEM((4, 4, 4, 32, CH), BF),
            pltpu.VMEM((2, 12 * PW, 2 * CH), BF),
            pltpu.VMEM((4, 256, CH), F32),
        ],
        compiler_params=params(24),
        cost_estimate=cost(2 * 2**30, 10 * 2**20),
        name="decode",
    )(where, own, other, w_in, b_in.reshape(1, CH), w_out, b_out.reshape(1, CH))


def around():
    pairs = []
    for core, step in ((0, 1), (1, -1)):
        for z in range(8):
            to = (z + step) % 8
            pairs.append(((z % 4) * 4 + core * 2 + z // 4, (to % 4) * 4 + core * 2 + to // 4))
    return pairs


def swapped(value, axes):
    return lax.all_to_all(value, axes, split_axis=0, concat_axis=0, tiled=True)


def hop(value):
    return lax.ppermute(value, STACK, around())


def across(value):
    return lax.ppermute(value, "core", [(0, 1), (1, 0)])


def shards(queries, keys, values, w_final, w_in, b_in, w_out, b_out):
    seq = lax.axis_index(("zl", "core")).astype(jnp.int32)
    tile = lax.axis_index(("y", "zh", "x")).astype(jnp.int32)
    where = jnp.stack([seq, tile])
    mixed = swapped(pack(queries, keys, values, w_final), PLANE)
    mine = mixed[:, 0:MSG]
    own_q = mixed[:, MSG:].reshape(PLANE_TOK, HD)
    both_q = jnp.stack([own_q, across(own_q)])
    state = attend(both_q, mine, None)
    coming = [hop(mine), hop(across(mine))]
    for step in range(6):
        message, state, where = lax.optimization_barrier((coming.pop(0), state, where))
        if step < 5:
            coming.append(hop(message))
        state = attend(both_q, message, state)
    message, state = lax.optimization_barrier((coming.pop(0), state))
    theirs = attend(both_q[1:2], message, state[1:2])
    theirs, kept_q, kept = lax.optimization_barrier((theirs, both_q[0:1], state[0:1]))
    crossed = across(theirs[0])
    ours = attend(kept_q, message, kept)
    parts = swapped(join(ours[0], crossed), PLANE)
    patch = swapped(patches(parts), RING)
    return decode(where, patch, across(patch), w_in, b_in, w_out, b_out).reshape(2, 128, 4, CH)


def solution(mesh):
    fine = Mesh(mesh.devices.reshape(SIZES), AXES)
    tokens = P(AXES, None)
    placed = (tokens, tokens, tokens, P(), P(), P(), P(), P())
    return jax.shard_map(
        shards,
        mesh=fine,
        in_specs=placed,
        out_specs=P(("zl", "core"), None, ("y", "zh", "x"), None),
        check_vma=False,
    )
```

```python
import functools
import math

import jax
import jax.numpy as jnp
from jax import lax
from jax.experimental import pallas as pl
from jax.experimental.pallas import tpu as pltpu
from jax.sharding import Mesh, PartitionSpec as P

AXES = ("zl", "core", "y", "zh", "x")
SIZES = (4, 2, 4, 2, 4)
PLANE = ("y", "x")
STACK = ("zl", "core", "zh")
RING = ("zl", "zh")

HEADS = 16
HD = 128
PW = 64
CH = 256
TOK = 64
MSG = 96
PLANE_TOK = 1024
SCALE = math.log2(math.e) / math.sqrt(HD)
BF = jnp.bfloat16
F32 = jnp.float32


def params(mib):
    return pltpu.CompilerParams(vmem_limit_bytes=mib * 2**20)


def cost(flops, moved):
    return pl.CostEstimate(flops=flops, bytes_accessed=moved, transcendentals=0)


def pack_kernel(q_hbm, k_hbm, v_hbm, w_hbm, out_ref, q_ref, k_ref, v_ref, w_ref, sems):
    moves = [
        pltpu.make_async_copy(source, target, sems.at[i])
        for i, (source, target) in enumerate(
            ((v_hbm, v_ref), (w_hbm, w_ref), (k_hbm, k_ref), (q_hbm, q_ref))
        )
    ]
    for move in moves:
        move.start()
    for move in moves[:2]:
        move.wait()
    for head in range(HEADS):
        lanes = pl.ds(head * HD, HD)
        small = lax.dot_general(
            v_ref[:, lanes], w_ref[:, lanes], (((1,), (1,)), ((), ())), preferred_element_type=F32
        )
        packed = jnp.concatenate([small[: TOK // 2], small[TOK // 2 :]], axis=1)
        out_ref[head, TOK:MSG] = packed.astype(BF)
    for move in moves[2:]:
        move.wait()
    for head in range(HEADS):
        lanes = pl.ds(head * HD, HD)
        out_ref[head, 0:TOK] = k_ref[:, lanes]
        out_ref[head, MSG : MSG + TOK] = q_ref[:, lanes]


def pack(queries, keys, values, w_final):
    return pl.pallas_call(
        pack_kernel,
        in_specs=[pl.BlockSpec(memory_space=pl.ANY)] * 4,
        out_shape=jax.ShapeDtypeStruct((HEADS, MSG + TOK, HD), BF),
        scratch_shapes=[pltpu.VMEM((TOK, HEADS * HD), BF)] * 3
        + [pltpu.VMEM((PW, HEADS * HD), BF), pltpu.SemaphoreType.DMA((4,))],
        compiler_params=params(60),
        cost_estimate=cost(2 * TOK * HEADS * HD * PW, 2**20),
        name="pack",
    )(queries, keys, values, w_final.T)


def attend_kernel(first, *refs):
    q_ref, kv_ref = refs[:2]
    old_ref = None if first else refs[2]
    new_ref, trial_ref, peak_ref = refs[-3:]
    sources = kv_ref.shape[0]

    def chunk(begin, count):
        rows = count * TOK
        keys = kv_ref[pl.ds(begin, count), 0:TOK, :].reshape(rows, HD)
        packed = kv_ref[pl.ds(begin, count), TOK:MSG, :]
        small = jnp.concatenate([packed[:, :, :PW], packed[:, :, PW:]], axis=1).reshape(rows, PW)
        return keys, jnp.concatenate([small, jnp.ones_like(small)], axis=1)

    def scores(keys, q):
        s = lax.dot_general(keys, q, (((1,), (1,)), ((), ())), preferred_element_type=F32)
        return s.reshape(s.shape[0] // 8, 8, s.shape[1]) * SCALE

    def weighted(s, shift, wide):
        p = jnp.exp2(s - shift[None])
        p = p.reshape(s.shape[0] * 8, s.shape[2]).astype(BF)
        u = lax.dot_general(wide, p, (((0,), (0,)), ((), ())), preferred_element_type=F32)
        return u[PW : PW + 8], u[:PW]

    def raise_peak(side, count):
        def more(i, _):
            s = scores(chunk(2 * i, 2)[0], q_ref[side])
            top = jnp.max(jnp.max(s, axis=0), axis=0, keepdims=True)
            peak_ref[...] = jnp.maximum(peak_ref[...], top)
            return 0

        lax.fori_loop(0, count // 2, more, 0)

    def attempt(side, largest):
        q = q_ref[side]
        if first:
            peak_ref[...] = jnp.full(peak_ref.shape, -jnp.inf, F32)
            raise_peak(side, 8)
            shift = peak_ref[...]
            total = jnp.zeros_like(shift)
            summed = jnp.zeros((PW, shift.shape[1]), F32)
        else:
            summed = old_ref[side, 0:PW]
            total = old_ref[side, PW : PW + 8]
            shift = old_ref[side, PW + 8 : PW + 16]
        fresh = jnp.zeros_like(total)
        for begin in range(0, sources, 8):
            keys, wide = chunk(begin, 8)
            t, u = weighted(scores(keys, q), shift, wide)
            fresh = fresh + t
            summed = summed + u
        trial_ref[side, 0:PW] = summed
        trial_ref[side, PW : PW + 8] = total + fresh
        trial_ref[side, PW + 8 : PW + 16] = shift
        return jnp.maximum(largest, jnp.max(fresh))

    largest = lax.fori_loop(0, q_ref.shape[0], attempt, jnp.float32(0))
    within = largest <= 2.0**100

    @pl.when(within)
    def _():
        new_ref[...] = trial_ref[...]

    @pl.when(jnp.logical_not(within))
    def _():
        def again(side, _):
            if first:
                new_ref[side] = jnp.zeros(new_ref.shape[1:], F32)
                shift = trial_ref[side, PW + 8 : PW + 16]
            else:
                new_ref[side] = old_ref[side]
                shift = new_ref[side, PW + 8 : PW + 16]
            peak_ref[...] = shift
            raise_peak(side, sources)
            top = peak_ref[...]
            shrink = jnp.exp2(shift - top)
            new_ref[side, 0:PW] = new_ref[side, 0:PW] * shrink[0:1]
            new_ref[side, PW : PW + 8] = new_ref[side, PW : PW + 8] * shrink
            new_ref[side, PW + 8 : PW + 16] = top

            def more(i, _):
                keys, wide = chunk(2 * i, 2)
                t, u = weighted(scores(keys, q_ref[side]), top, wide)
                new_ref[side, 0:PW] += u
                new_ref[side, PW : PW + 8] += t
                return 0

            return lax.fori_loop(0, sources // 2, more, 0)

        lax.fori_loop(0, q_ref.shape[0], again, 0)


def attend(queries, message, state):
    first = state is None
    operands = [queries, message] + ([] if first else [state])
    rows = message.shape[0] * TOK
    sides = queries.shape[0]
    return pl.pallas_call(
        functools.partial(attend_kernel, first),
        out_shape=jax.ShapeDtypeStruct((sides, PW + 16, PLANE_TOK), F32),
        scratch_shapes=[
            pltpu.VMEM((sides, PW + 16, PLANE_TOK), F32),
            pltpu.VMEM((8, PLANE_TOK), F32),
        ],
        input_output_aliases={} if first else {2: 0},
        compiler_params=params(20),
        cost_estimate=cost(2 * sides * PLANE_TOK * rows * 2 * HD, sides * 2**20),
        name="attend",
    )(*operands)


def join_kernel(mine_ref, other_ref, out_ref, rows_ref):
    top = jnp.maximum(mine_ref[PW + 8 : PW + 16], other_ref[PW + 8 : PW + 16])
    one = jnp.exp2(mine_ref[PW + 8 : PW + 16] - top)
    two = jnp.exp2(other_ref[PW + 8 : PW + 16] - top)
    total = mine_ref[PW : PW + 8] * one + other_ref[PW : PW + 8] * two
    summed = mine_ref[0:PW] * one[0:1] + other_ref[0:PW] * two[0:1]
    share = summed / total[0:1]
    rows_ref[:, 0:PW] = jnp.transpose(share)
    none = jnp.zeros((32, PW), F32)
    columns = [rows_ref[pl.ds(c, 32, stride=32), 0:PW] for c in range(32)]

    def column(c):
        return columns[c] if 0 <= c < 32 else none

    for y in range(4):
        for x in range(4):
            for j in range(3):
                c = y * 8 + x - 1 + j
                both = jnp.concatenate([column(c), column(c + 4)], axis=1)
                out_ref[y * 4 + x, j] = both.astype(BF)


def join(mine, other):
    return pl.pallas_call(
        join_kernel,
        out_shape=jax.ShapeDtypeStruct((16, 3, 32, 2 * PW), BF),
        scratch_shapes=[pltpu.VMEM((PLANE_TOK, 2 * PW), F32)],
        compiler_params=params(24),
        cost_estimate=cost(2**20, 2**20),
        name="join",
    )(mine, other)


def patch_kernel(in_ref, out_ref):
    total = in_ref[0].astype(F32)
    for head in range(1, HEADS):
        total = total + in_ref[head].astype(F32)
    for strip in range(2):
        part = total[:, :, strip * PW : (strip + 1) * PW]
        flat = jnp.concatenate([part[:, 0:16], part[:, 16:32]], axis=2).astype(BF)
        for group in range(4):
            out_ref[2 * group + strip] = flat


def patches(parts):
    return pl.pallas_call(
        patch_kernel,
        out_shape=jax.ShapeDtypeStruct((8, 3, 16, 2 * PW), BF),
        compiler_params=params(24),
        cost_estimate=cost(2**19, 2**19),
        name="patch_sum",
    )(parts)


def spread_w_in(w_ref, w1_ref):
    none = jnp.zeros((16, CH), BF)
    for a in range(2):
        for b in range(2):
            for near in range(4):
                for beside in range(4):
                    dy, dx = near - 1 + a, beside - 1 + b
                    place = ((near // 2) * 2 + beside // 2) * PW + ((near % 2) * 2 + beside % 2) * 16
                    for dt in range(3):
                        known = 0 <= dy < 3 and 0 <= dx < 3
                        tap = w_ref[dt, dy, dx] if known else none
                        rows = pl.ds(dt * 4 * PW + place, 16)
                        w1_ref[a, rows, b * CH : (b + 1) * CH] = tap


PICKS = {(0, 0): (0,), (0, 1): (1, 2), (1, 0): (0, 1), (1, 1): (2,)}


def upsampled_conv(w_ref, act_ref, sum_ref):
    for p in range(2):
        totals = [None, None]
        for dt in range(3):
            for i in range(2):
                rows = []
                for dx in range(3):
                    row = w_ref[dt, PICKS[p, i][0], dx].astype(F32)
                    for dy in PICKS[p, i][1:]:
                        row = row + w_ref[dt, dy, dx].astype(F32)
                    rows.append(row)
                for q in range(2):
                    for j in range(2):
                        tap = rows[PICKS[q, j][0]]
                        for dx in PICKS[q, j][1:]:
                            tap = tap + rows[dx]
                        blocks = []
                        for a in range(2):
                            view = act_ref[a + p + i, dt : dt + 2, q + j : q + j + 2]
                            blocks.append(view.reshape(128, CH))
                        lhs = jnp.concatenate(blocks, axis=0)
                        part = jnp.dot(lhs, tap.astype(BF), preferred_element_type=F32)
                        totals[q] = part if totals[q] is None else totals[q] + part
        for q in range(2):
            sum_ref[2 * p + q] = totals[q]


def decode_kernel(
    where_ref, own_ref, other_ref, w_in_ref, b1_ref, w_out_ref, b2_ref, out_ref, act_ref, w1_ref, sum_ref
):
    spread_w_in(w_in_ref, w1_ref)
    seq = where_ref[0]
    tile = where_ref[1]
    tokens = []
    for back in (2, 1, 0):
        chip = jnp.maximum(seq - back, 0) >> 1
        known = (seq >= back).astype(F32)
        in_ref = other_ref if back == 1 else own_ref
        halves = [in_ref[2 * chip + zh].astype(F32) * known for zh in range(2)]
        for frame in range(2):
            lanes = slice(frame * PW, (frame + 1) * PW)
            columns = []
            for j in range(3):
                pieces = []
                for high in range(2):
                    for zh in range(2):
                        pieces.append(halves[zh][j, high * 8 : (high + 1) * 8, lanes])
                columns.append(jnp.concatenate(pieces, axis=0))
            tokens.append(columns)
    blank = jnp.zeros((1, 2 * PW), F32)
    views = {}
    for frame in range(6):
        for side in range(2):
            both = jnp.concatenate([tokens[frame][side], tokens[frame][side + 1]], axis=1)
            views[frame, side, 0] = both.astype(BF)
            views[frame, side, -1] = jnp.concatenate([blank, both[:-1]], axis=0).astype(BF)
            views[frame, side, 1] = jnp.concatenate([both[1:], blank], axis=0).astype(BF)

    blank = jnp.zeros((1, CH), F32)
    first = {}
    for a in range(2):
        for side in range(2):
            rows = []
            for frame in range(4):
                row = []
                for dt in range(3):
                    for near in range(2):
                        row.append(views[frame + dt, side, a - 1 + near])
                rows.append(jnp.concatenate(row, axis=1))
            lhs = jnp.concatenate(rows, axis=0)
            got = jnp.dot(lhs, w1_ref[a], preferred_element_type=F32)
            for half in range(2):
                column = 2 * side + half
                b = 1 - half
                first[a, column] = (got[:, b * CH : (b + 1) * CH] + b1_ref[...]).astype(BF)

    for column in range(4):
        inside = 1.0
        if column == 0:
            inside = (tile > 0).astype(F32)
        if column == 3:
            inside = (tile < 31).astype(F32)
        for a in range(2):
            full = first[a, column].astype(F32)
            active = full / (1.0 + jnp.exp(-full))
            for frame in range(4):
                keep = inside * ((seq > 0).astype(F32) if frame < 2 else 1.0)
                part = active[frame * 32 : (frame + 1) * 32] * keep
                if a == 0:
                    act_ref[1, frame, column] = part.astype(BF)
                    act_ref[3, frame, column] = jnp.concatenate([part[1:], blank], 0).astype(BF)
                else:
                    act_ref[2, frame, column] = part.astype(BF)
                    act_ref[0, frame, column] = jnp.concatenate([blank, part[:-1]], 0).astype(BF)

    upsampled_conv(w_out_ref, act_ref, sum_ref)
    to = lax.broadcasted_iota(jnp.int32, (256, 128), 0)
    source = lax.broadcasted_iota(jnp.int32, (256, 128), 1)
    order = jnp.where((to & 7) * 32 + (to >> 3) == source, 1.0, 0.0).astype(BF)
    for frame in range(2):
        for a in range(2):
            for p in range(2):
                columns = []
                for x in range(4):
                    column, q = x // 2, x % 2
                    start = (a * 4 + frame * 2 + column) * 32
                    skip = first[a, column + 1][(frame + 2) * 32 : (frame + 3) * 32].astype(F32)
                    columns.append(skip + sum_ref[2 * p + q, start : start + 32] + b2_ref[...])
                stacked = jnp.concatenate(columns, axis=0).astype(BF)
                rows = jnp.dot(order, stacked, preferred_element_type=F32)
                out_ref[frame, :, 2 * a + p] = rows.reshape(32, 8, CH)[:, 0:4].astype(BF)


def decode(where, own, other, w_in, b_in, w_out, b_out):
    vmem = pl.BlockSpec(memory_space=pltpu.VMEM)
    return pl.pallas_call(
        decode_kernel,
        in_specs=[pl.BlockSpec(memory_space=pltpu.SMEM)] + [vmem] * 6,
        out_specs=vmem,
        out_shape=jax.ShapeDtypeStruct((2, 32, 4, 4, CH), BF),
        scratch_shapes=[
            pltpu.VMEM((4, 4, 4, 32, CH), BF),
            pltpu.VMEM((2, 12 * PW, 2 * CH), BF),
            pltpu.VMEM((4, 256, CH), F32),
        ],
        compiler_params=params(24),
        cost_estimate=cost(2 * 2**30, 10 * 2**20),
        name="decode",
    )(where, own, other, w_in, b_in.reshape(1, CH), w_out, b_out.reshape(1, CH))


def around():
    pairs = []
    for core, step in ((0, -1), (1, 1)):
        for z in range(8):
            to = (z + step) % 8
            pairs.append(((z % 4) * 4 + core * 2 + z // 4, (to % 4) * 4 + core * 2 + to // 4))
    return pairs


def swapped(value, axes):
    return lax.all_to_all(value, axes, split_axis=0, concat_axis=0, tiled=True)


def hop(value):
    return lax.ppermute(value, STACK, around())


def across(value):
    return lax.ppermute(value, "core", [(0, 1), (1, 0)])


def shards(queries, keys, values, w_final, w_in, b_in, w_out, b_out):
    seq = lax.axis_index(("zl", "core")).astype(jnp.int32)
    tile = lax.axis_index(("y", "zh", "x")).astype(jnp.int32)
    where = jnp.stack([seq, tile])
    mixed = swapped(pack(queries, keys, values, w_final), PLANE)
    mine = mixed[:, 0:MSG]
    own_q = mixed[:, MSG:].reshape(PLANE_TOK, HD)
    both_q = jnp.stack([own_q, across(own_q)])
    state = attend(both_q, mine, None)
    coming = [hop(mine), hop(across(mine))]
    for step in range(6):
        message, state, where = lax.optimization_barrier((coming.pop(0), state, where))
        if step < 5:
            coming.append(hop(message))
        state = attend(both_q, message, state)
    message, state = lax.optimization_barrier((coming.pop(0), state))
    theirs = attend(both_q[1:2], message, state[1:2])
    theirs, kept_q, kept = lax.optimization_barrier((theirs, both_q[0:1], state[0:1]))
    crossed = across(theirs[0])
    ours = attend(kept_q, message, kept)
    parts = swapped(join(ours[0], crossed), PLANE)
    patch = swapped(patches(parts), RING)
    return decode(where, patch, across(patch), w_in, b_in, w_out, b_out).reshape(2, 128, 4, CH)


def solution(mesh):
    fine = Mesh(mesh.devices.reshape(SIZES), AXES)
    tokens = P(AXES, None)
    placed = (tokens, tokens, tokens, P(), P(), P(), P(), P())
    return jax.shard_map(
        shards,
        mesh=fine,
        in_specs=placed,
        out_specs=P(("zl", "core"), None, ("y", "zh", "x"), None),
        check_vma=False,
    )
```

```python
import functools
import math

import jax
import jax.numpy as jnp
from jax import lax
from jax.experimental import pallas as pl
from jax.experimental.pallas import tpu as pltpu
from jax.sharding import Mesh, PartitionSpec as P

AXES = ("zl", "core", "y", "zh", "x")
SIZES = (4, 2, 4, 2, 4)
PLANE = ("y", "x")
STACK = ("zl", "core", "zh")
RING = ("zl", "zh")

HEADS = 16
HD = 128
PW = 64
CH = 256
TOK = 64
MSG = 96
PLANE_TOK = 1024
SCALE = math.log2(math.e) / math.sqrt(HD)
BF = jnp.bfloat16
F32 = jnp.float32


def params(mib):
    return pltpu.CompilerParams(vmem_limit_bytes=mib * 2**20)


def cost(flops, moved):
    return pl.CostEstimate(flops=flops, bytes_accessed=moved, transcendentals=0)


def pack_kernel(q_hbm, k_hbm, v_hbm, w_hbm, out_ref, q_ref, k_ref, v_ref, w_ref, sems):
    moves = [
        pltpu.make_async_copy(source, target, sems.at[i])
        for i, (source, target) in enumerate(
            ((v_hbm, v_ref), (w_hbm, w_ref), (k_hbm, k_ref), (q_hbm, q_ref))
        )
    ]
    for move in moves:
        move.start()
    for move in moves[:2]:
        move.wait()
    for head in range(HEADS):
        lanes = pl.ds(head * HD, HD)
        small = lax.dot_general(
            v_ref[:, lanes], w_ref[:, lanes], (((1,), (1,)), ((), ())), preferred_element_type=F32
        )
        packed = jnp.concatenate([small[: TOK // 2], small[TOK // 2 :]], axis=1)
        out_ref[head, TOK:MSG] = packed.astype(BF)
    for move in moves[2:]:
        move.wait()
    for head in range(HEADS):
        lanes = pl.ds(head * HD, HD)
        out_ref[head, 0:TOK] = k_ref[:, lanes]
        out_ref[head, MSG : MSG + TOK] = q_ref[:, lanes]


def pack(queries, keys, values, w_final):
    return pl.pallas_call(
        pack_kernel,
        in_specs=[pl.BlockSpec(memory_space=pl.ANY)] * 4,
        out_shape=jax.ShapeDtypeStruct((HEADS, MSG + TOK, HD), BF),
        scratch_shapes=[pltpu.VMEM((TOK, HEADS * HD), BF)] * 3
        + [pltpu.VMEM((PW, HEADS * HD), BF), pltpu.SemaphoreType.DMA((4,))],
        compiler_params=params(60),
        cost_estimate=cost(2 * TOK * HEADS * HD * PW, 2**20),
        name="pack",
    )(queries, keys, values, w_final.T)


def attend_kernel(first, *refs):
    q_ref, kv_ref = refs[:2]
    old_ref = None if first else refs[2]
    new_ref, trial_ref, peak_ref = refs[-3:]
    sources = kv_ref.shape[0]

    def chunk(begin, count):
        rows = count * TOK
        keys = kv_ref[pl.ds(begin, count), 0:TOK, :].reshape(rows, HD)
        packed = kv_ref[pl.ds(begin, count), TOK:MSG, :]
        small = jnp.concatenate([packed[:, :, :PW], packed[:, :, PW:]], axis=1).reshape(rows, PW)
        return keys, jnp.concatenate([small, jnp.ones_like(small)], axis=1)

    def scores(keys, q):
        s = lax.dot_general(keys, q, (((1,), (1,)), ((), ())), preferred_element_type=F32)
        return s.reshape(s.shape[0] // 8, 8, s.shape[1]) * SCALE

    def weighted(s, shift, wide):
        p = jnp.exp2(s - shift[None])
        p = p.reshape(s.shape[0] * 8, s.shape[2]).astype(BF)
        u = lax.dot_general(wide, p, (((0,), (0,)), ((), ())), preferred_element_type=F32)
        return u[PW : PW + 8], u[:PW]

    def raise_peak(side, count):
        def more(i, _):
            s = scores(chunk(2 * i, 2)[0], q_ref[side])
            top = jnp.max(jnp.max(s, axis=0), axis=0, keepdims=True)
            peak_ref[...] = jnp.maximum(peak_ref[...], top)
            return 0

        lax.fori_loop(0, count // 2, more, 0)

    def attempt(side, largest):
        q = q_ref[side]
        if first:
            peak_ref[...] = jnp.full(peak_ref.shape, -jnp.inf, F32)
            raise_peak(side, 8)
            shift = peak_ref[...]
            total = jnp.zeros_like(shift)
            summed = jnp.zeros((PW, shift.shape[1]), F32)
        else:
            summed = old_ref[side, 0:PW]
            total = old_ref[side, PW : PW + 8]
            shift = old_ref[side, PW + 8 : PW + 16]
        fresh = jnp.zeros_like(total)
        for begin in range(0, sources, 8):
            keys, wide = chunk(begin, 8)
            t, u = weighted(scores(keys, q), shift, wide)
            fresh = fresh + t
            summed = summed + u
        trial_ref[side, 0:PW] = summed
        trial_ref[side, PW : PW + 8] = total + fresh
        trial_ref[side, PW + 8 : PW + 16] = shift
        return jnp.maximum(largest, jnp.max(fresh))

    largest = lax.fori_loop(0, q_ref.shape[0], attempt, jnp.float32(0))
    within = largest <= 2.0**100

    @pl.when(within)
    def _():
        new_ref[...] = trial_ref[...]

    @pl.when(jnp.logical_not(within))
    def _():
        def again(side, _):
            if first:
                new_ref[side] = jnp.zeros(new_ref.shape[1:], F32)
                shift = trial_ref[side, PW + 8 : PW + 16]
            else:
                new_ref[side] = old_ref[side]
                shift = new_ref[side, PW + 8 : PW + 16]
            peak_ref[...] = shift
            raise_peak(side, sources)
            top = peak_ref[...]
            shrink = jnp.exp2(shift - top)
            new_ref[side, 0:PW] = new_ref[side, 0:PW] * shrink[0:1]
            new_ref[side, PW : PW + 8] = new_ref[side, PW : PW + 8] * shrink
            new_ref[side, PW + 8 : PW + 16] = top

            def more(i, _):
                keys, wide = chunk(2 * i, 2)
                t, u = weighted(scores(keys, q_ref[side]), top, wide)
                new_ref[side, 0:PW] += u
                new_ref[side, PW : PW + 8] += t
                return 0

            return lax.fori_loop(0, sources // 2, more, 0)

        lax.fori_loop(0, q_ref.shape[0], again, 0)


def attend(queries, message, state):
    first = state is None
    operands = [queries, message] + ([] if first else [state])
    rows = message.shape[0] * TOK
    sides = queries.shape[0]
    return pl.pallas_call(
        functools.partial(attend_kernel, first),
        out_shape=jax.ShapeDtypeStruct((sides, PW + 16, PLANE_TOK), F32),
        scratch_shapes=[
            pltpu.VMEM((sides, PW + 16, PLANE_TOK), F32),
            pltpu.VMEM((8, PLANE_TOK), F32),
        ],
        input_output_aliases={} if first else {2: 0},
        compiler_params=params(20),
        cost_estimate=cost(2 * sides * PLANE_TOK * rows * 2 * HD, sides * 2**20),
        name="attend",
    )(*operands)


def join_kernel(mine_ref, other_ref, out_ref, rows_ref):
    top = jnp.maximum(mine_ref[PW + 8 : PW + 16], other_ref[PW + 8 : PW + 16])
    one = jnp.exp2(mine_ref[PW + 8 : PW + 16] - top)
    two = jnp.exp2(other_ref[PW + 8 : PW + 16] - top)
    total = mine_ref[PW : PW + 8] * one + other_ref[PW : PW + 8] * two
    summed = mine_ref[0:PW] * one[0:1] + other_ref[0:PW] * two[0:1]
    share = summed / total[0:1]
    rows_ref[:, 0:PW] = jnp.transpose(share)
    none = jnp.zeros((32, PW), F32)
    columns = [rows_ref[pl.ds(c, 32, stride=32), 0:PW] for c in range(32)]

    def column(c):
        return columns[c] if 0 <= c < 32 else none

    for y in range(4):
        for x in range(4):
            for j in range(3):
                c = y * 8 + x - 1 + j
                both = jnp.concatenate([column(c), column(c + 4)], axis=1)
                out_ref[y * 4 + x, j] = both.astype(BF)


def join(mine, other):
    return pl.pallas_call(
        join_kernel,
        out_shape=jax.ShapeDtypeStruct((16, 3, 32, 2 * PW), BF),
        scratch_shapes=[pltpu.VMEM((PLANE_TOK, 2 * PW), F32)],
        compiler_params=params(24),
        cost_estimate=cost(2**20, 2**20),
        name="join",
    )(mine, other)


def patch_kernel(in_ref, out_ref):
    total = in_ref[0].astype(F32)
    for head in range(1, HEADS):
        total = total + in_ref[head].astype(F32)
    for strip in range(2):
        part = total[:, :, strip * PW : (strip + 1) * PW]
        flat = jnp.concatenate([part[:, 0:16], part[:, 16:32]], axis=2).astype(BF)
        for group in range(4):
            out_ref[2 * group + strip] = flat


def patches(parts):
    return pl.pallas_call(
        patch_kernel,
        out_shape=jax.ShapeDtypeStruct((8, 3, 16, 2 * PW), BF),
        compiler_params=params(24),
        cost_estimate=cost(2**19, 2**19),
        name="patch_sum",
    )(parts)


def spread_w_in(w_ref, w1_ref):
    none = jnp.zeros((16, CH), BF)
    for a in range(2):
        for b in range(2):
            for near in range(4):
                for beside in range(4):
                    dy, dx = near - 1 + a, beside - 1 + b
                    place = ((near // 2) * 2 + beside // 2) * PW + ((near % 2) * 2 + beside % 2) * 16
                    for dt in range(3):
                        known = 0 <= dy < 3 and 0 <= dx < 3
                        tap = w_ref[dt, dy, dx] if known else none
                        rows = pl.ds(dt * 4 * PW + place, 16)
                        w1_ref[a, rows, b * CH : (b + 1) * CH] = tap


PICKS = {(0, 0): (0,), (0, 1): (1, 2), (1, 0): (0, 1), (1, 1): (2,)}


def upsampled_conv(w_ref, act_ref, sum_ref):
    for p in range(2):
        totals = [None, None]
        for dt in range(3):
            for i in range(2):
                rows = []
                for dx in range(3):
                    row = w_ref[dt, PICKS[p, i][0], dx].astype(F32)
                    for dy in PICKS[p, i][1:]:
                        row = row + w_ref[dt, dy, dx].astype(F32)
                    rows.append(row)
                for q in range(2):
                    for j in range(2):
                        tap = rows[PICKS[q, j][0]]
                        for dx in PICKS[q, j][1:]:
                            tap = tap + rows[dx]
                        blocks = []
                        for a in range(2):
                            view = act_ref[a + p + i, dt : dt + 2, q + j : q + j + 2]
                            blocks.append(view.reshape(128, CH))
                        lhs = jnp.concatenate(blocks, axis=0)
                        part = jnp.dot(lhs, tap.astype(BF), preferred_element_type=F32)
                        totals[q] = part if totals[q] is None else totals[q] + part
        for q in range(2):
            sum_ref[2 * p + q] = totals[q]


def decode_kernel(
    where_ref, own_ref, other_ref, w_in_ref, b1_ref, w_out_ref, b2_ref, out_ref, act_ref, w1_ref, sum_ref
):
    spread_w_in(w_in_ref, w1_ref)
    seq = where_ref[0]
    tile = where_ref[1]
    tokens = []
    for back in (2, 1, 0):
        chip = jnp.maximum(seq - back, 0) >> 1
        known = (seq >= back).astype(F32)
        in_ref = other_ref if back == 1 else own_ref
        halves = [in_ref[2 * chip + zh].astype(F32) * known for zh in range(2)]
        for frame in range(2):
            lanes = slice(frame * PW, (frame + 1) * PW)
            columns = []
            for j in range(3):
                pieces = []
                for high in range(2):
                    for zh in range(2):
                        pieces.append(halves[zh][j, high * 8 : (high + 1) * 8, lanes])
                columns.append(jnp.concatenate(pieces, axis=0))
            tokens.append(columns)
    blank = jnp.zeros((1, 2 * PW), F32)
    views = {}
    for frame in range(6):
        for side in range(2):
            both = jnp.concatenate([tokens[frame][side], tokens[frame][side + 1]], axis=1)
            views[frame, side, 0] = both.astype(BF)
            views[frame, side, -1] = jnp.concatenate([blank, both[:-1]], axis=0).astype(BF)
            views[frame, side, 1] = jnp.concatenate([both[1:], blank], axis=0).astype(BF)

    blank = jnp.zeros((1, CH), F32)
    first = {}
    for a in range(2):
        for side in range(2):
            rows = []
            for frame in range(4):
                row = []
                for dt in range(3):
                    for near in range(2):
                        row.append(views[frame + dt, side, a - 1 + near])
                rows.append(jnp.concatenate(row, axis=1))
            lhs = jnp.concatenate(rows, axis=0)
            got = jnp.dot(lhs, w1_ref[a], preferred_element_type=F32)
            for half in range(2):
                column = 2 * side + half
                b = 1 - half
                first[a, column] = (got[:, b * CH : (b + 1) * CH] + b1_ref[...]).astype(BF)

    for column in range(4):
        inside = 1.0
        if column == 0:
            inside = (tile > 0).astype(F32)
        if column == 3:
            inside = (tile < 31).astype(F32)
        for a in range(2):
            full = first[a, column].astype(F32)
            active = full / (1.0 + jnp.exp(-full))
            for frame in range(4):
                keep = inside * ((seq > 0).astype(F32) if frame < 2 else 1.0)
                part = active[frame * 32 : (frame + 1) * 32] * keep
                if a == 0:
                    act_ref[1, frame, column] = part.astype(BF)
                    act_ref[3, frame, column] = jnp.concatenate([part[1:], blank], 0).astype(BF)
                else:
                    act_ref[2, frame, column] = part.astype(BF)
                    act_ref[0, frame, column] = jnp.concatenate([blank, part[:-1]], 0).astype(BF)

    upsampled_conv(w_out_ref, act_ref, sum_ref)
    to = lax.broadcasted_iota(jnp.int32, (256, 128), 0)
    source = lax.broadcasted_iota(jnp.int32, (256, 128), 1)
    order = jnp.where((to & 7) * 32 + (to >> 3) == source, 1.0, 0.0).astype(BF)
    for frame in range(2):
        for a in range(2):
            for p in range(2):
                columns = []
                for x in range(4):
                    column, q = x // 2, x % 2
                    start = (a * 4 + frame * 2 + column) * 32
                    skip = first[a, column + 1][(frame + 2) * 32 : (frame + 3) * 32].astype(F32)
                    columns.append(skip + sum_ref[2 * p + q, start : start + 32] + b2_ref[...])
                stacked = jnp.concatenate(columns, axis=0).astype(BF)
                rows = jnp.dot(order, stacked, preferred_element_type=F32)
                out_ref[frame, :, 2 * a + p] = rows.reshape(32, 8, CH)[:, 0:4].astype(BF)


def decode(where, own, other, w_in, b_in, w_out, b_out):
    vmem = pl.BlockSpec(memory_space=pltpu.VMEM)
    return pl.pallas_call(
        decode_kernel,
        in_specs=[pl.BlockSpec(memory_space=pltpu.SMEM)] + [vmem] * 6,
        out_specs=vmem,
        out_shape=jax.ShapeDtypeStruct((2, 32, 4, 4, CH), BF),
        scratch_shapes=[
            pltpu.VMEM((4, 4, 4, 32, CH), BF),
            pltpu.VMEM((2, 12 * PW, 2 * CH), BF),
            pltpu.VMEM((4, 256, CH), F32),
        ],
        compiler_params=params(24),
        cost_estimate=cost(2 * 2**30, 10 * 2**20),
        name="decode",
    )(where, own, other, w_in, b_in.reshape(1, CH), w_out, b_out.reshape(1, CH))


def around():
    pairs = []
    for core, step in ((0, -1), (1, 1)):
        for z in range(8):
            to = (z + step) % 8
            pairs.append(((z % 4) * 4 + core * 2 + z // 4, (to % 4) * 4 + core * 2 + to // 4))
    return pairs


def swapped(value, axes):
    return lax.all_to_all(value, axes, split_axis=0, concat_axis=0, tiled=True)


def hop(value):
    return lax.ppermute(value, STACK, around())


def across(value):
    return lax.ppermute(value, "core", [(0, 1), (1, 0)])


def shards(queries, keys, values, w_final, w_in, b_in, w_out, b_out):
    seq = lax.axis_index(("zl", "core")).astype(jnp.int32)
    tile = lax.axis_index(("y", "zh", "x")).astype(jnp.int32)
    where = jnp.stack([seq, tile])
    mixed = swapped(pack(queries, keys, values, w_final), PLANE)
    mine = mixed[:, 0:MSG]
    own_q = mixed[:, MSG:].reshape(PLANE_TOK, HD)
    both_q = jnp.stack([own_q, across(own_q)])
    state = attend(both_q, mine[0:8], None)
    other, state = lax.optimization_barrier((across(mine), state))
    coming = [hop(mine), hop(other)]
    state = attend(both_q, mine[8:16], state)
    for step in range(6):
        message, state, where = lax.optimization_barrier((coming.pop(0), state, where))
        if step < 5:
            coming.append(hop(message))
        state = attend(both_q, message, state)
    message, state = lax.optimization_barrier((coming.pop(0), state))
    theirs = attend(both_q[1:2], message, state[1:2])
    theirs, kept_q, kept = lax.optimization_barrier((theirs, both_q[0:1], state[0:1]))
    crossed = across(theirs[0])
    ours = attend(kept_q, message, kept)
    parts = swapped(join(ours[0], crossed), PLANE)
    patch = swapped(patches(parts), RING)
    return decode(where, patch, across(patch), w_in, b_in, w_out, b_out).reshape(2, 128, 4, CH)


def solution(mesh):
    fine = Mesh(mesh.devices.reshape(SIZES), AXES)
    tokens = P(AXES, None)
    placed = (tokens, tokens, tokens, P(), P(), P(), P(), P())
    return jax.shard_map(
        shards,
        mesh=fine,
        in_specs=placed,
        out_specs=P(("zl", "core"), None, ("y", "zh", "x"), None),
        check_vma=False,
    )
```
